256 devices in a mesh: ctxa: 8 (over z_hi, core), ctxb: 32 (over z_lo, y, x).
Axes of the slice: x: 4, y: 4, z: 8 (z_hi: 4, z_lo: 2; z = z_hi * 2 + z_lo), core: 2. Of those that a mesh axis runs over, the one named last changes fastest.
Arguments:
- queries: bfloat16 [32768, 512], P(('ctxa', 'ctxb')), may hold values from -8 to 8
- keys: bfloat16 [32768, 512], P(('ctxa', 'ctxb')), may hold values from -8 to 8
- values: bfloat16 [32768, 512], P(('ctxa', 'ctxb')), may hold values from -6 to 6
- grad_out: bfloat16 [32768, 512], P(('ctxa', 'ctxb')), may hold values from -48 to 48
- offsets: int32 [3, 8], replicated, may hold values from 0 to 31, as said below
Outputs:
- grad_queries: bfloat16 [32768, 512], P(('ctxa', 'ctxb'))
- grad_keys: bfloat16 [32768, 512], P(('ctxa', 'ctxb'))
- grad_values: bfloat16 [32768, 512], P(('ctxa', 'ctxb'))
The draws below stay inside these ranges and needn't reach their ends.
Inputs may be any that keep to these rules, and one draw needn't show every extreme that they name: offsets[l, h] is below the dilation of level l; at every level some head has the dilation minus one.
All inputs are finite; a program needn't handle non-finite values.
Results may differ from the reference program's by a relative error of at most 0.0093.
Values may be sent and summed in bfloat16 or wider, within the bound.
A program may use at most 128 MiB of HBM per device.

```python
import jax
import jax.numpy as jnp
from jax import lax

HEADS = 8
HEAD_DIM = 64
KEYS = 1024
LEVELS = 3
D = 512
TOKENS = 32768


def draw_queries(key, part):
    key = jax.random.fold_in(key, 3)
    return jnp.clip(jax.random.normal(key, (TOKENS, D), jnp.float32), -6.0, 6.0).astype(jnp.bfloat16)


def draw_keys(key, part):
    key = jax.random.fold_in(key, 5)
    return jnp.clip(jax.random.normal(key, (TOKENS, D), jnp.float32), -6.0, 6.0).astype(jnp.bfloat16)


def draw_offsets(key, part):
    key = jax.random.fold_in(key, 11)
    raw_key, head_key = jax.random.split(key)
    raw = jax.random.randint(raw_key, (LEVELS, HEADS), 0, 1 << 20)
    level_ids = jnp.arange(LEVELS, dtype=jnp.int32)
    dilations = jnp.where(level_ids == LEVELS - 1, TOKENS // KEYS, 2 ** level_ids).astype(jnp.int32)[:, None]
    drawn = raw % dilations
    marked = jax.random.randint(head_key, (LEVELS, 1), 0, HEADS)
    return jnp.where(jnp.arange(HEADS, dtype=jnp.int32)[None, :] == marked, dilations - 1, drawn).astype(jnp.int32)


def steps_of(stream_key, extent, cuts, least, high):
    def one(dim, blocks):
        steps = jax.random.uniform(jax.random.fold_in(jax.random.fold_in(stream_key, 6), dim), (blocks,), jnp.float32, least / len(cuts), high / len(cuts))
        return jnp.repeat(jnp.exp(steps), extent[dim] // blocks).reshape((-1,) + (1,) * (len(extent) - dim - 1))

    loudness = one(*cuts[0])
    for cut in cuts[1:]:
        loudness = loudness * one(*cut)
    return loudness


def gaussian(stream_key, shape, scale, limit, cuts=(), held_as=jnp.bfloat16):
    array = scale * jax.random.normal(stream_key, shape, jnp.float32)
    if cuts:
        array = array * steps_of(stream_key, shape, cuts, -0.22, 0.18)
    return jnp.clip(array, -limit, limit).astype(held_as)


def setup_inputs(seed: int = 0) -> dict:
    splits = jax.random.split(jax.random.key(seed), 6)
    return {
        "queries": draw_queries(jax.random.fold_in(splits[5], 71), 0),
        "keys": draw_keys(jax.random.fold_in(splits[5], 71), 0),
        "values": gaussian(splits[2], (TOKENS, D), 1.0, 6.0, ((0, 256),)),
        "grad_out": jnp.clip(jax.random.uniform(splits[3], (TOKENS, D), jnp.float32, -48.0, 48.0) * steps_of(splits[3], (TOKENS, D), ((0, 256),), -0.4, 0.0), -48.0, 48.0).astype(jnp.bfloat16),
        "offsets": draw_offsets(jax.random.fold_in(splits[5], 71), 0),
    }


def level_plan(level):
    if level == LEVELS - 1:
        dilation = TOKENS // KEYS
        segment = TOKENS
    else:
        dilation = 2 ** level
        segment = KEYS * dilation
    return dilation, segment // dilation, TOKENS // segment


def dilated_index(level, offsets, dilation):
    rows = jnp.arange(TOKENS // dilation, dtype=jnp.int32)[:, None] * dilation + offsets[level][None, :].astype(jnp.int32)
    heads = jnp.broadcast_to(jnp.arange(HEADS, dtype=jnp.int32)[None, :], rows.shape)
    return rows.astype(jnp.int32), heads


def segment_scores(query_sel, key_sel):
    return jnp.einsum('qhd,khd->hqk', query_sel.astype(jnp.float32), key_sel.astype(jnp.float32)) * HEAD_DIM ** -0.5


def segment_lse(pair):
    scores = segment_scores(pair[0], pair[1])
    highest = jnp.max(scores, axis=-1, keepdims=True)
    level_lse = (highest + jnp.log(jnp.sum(jnp.exp(scores - highest), axis=-1, keepdims=True)))[..., 0]
    return level_lse.T


def segment_output(items):
    query_sel, key_sel, value_sel, lse_sel = items
    scores = segment_scores(query_sel, key_sel)
    probs_low = jnp.exp(scores - lse_sel.T[..., None]).astype(jnp.bfloat16)
    return jnp.einsum('hqk,khd->qhd', probs_low.astype(jnp.float32), value_sel.astype(jnp.float32))


def segment_grads(items):
    query_sel, key_sel, value_sel, grad_sel, lse_sel, delta_sel = items
    scores = segment_scores(query_sel, key_sel)
    probs = jnp.exp(scores - lse_sel.T[..., None])
    probs_low = probs.astype(jnp.bfloat16)
    dprob = jnp.einsum('qhd,khd->hqk', grad_sel.astype(jnp.float32), value_sel.astype(jnp.float32))
    dscore = (probs * (dprob - delta_sel.T[..., None]) * HEAD_DIM ** -0.5).astype(jnp.bfloat16)
    part_q = jnp.einsum('hqk,khd->qhd', dscore.astype(jnp.float32), key_sel.astype(jnp.float32))
    part_k = jnp.einsum('hqk,qhd->khd', dscore.astype(jnp.float32), query_sel.astype(jnp.float32))
    part_v = jnp.einsum('hqk,qhd->khd', probs_low.astype(jnp.float32), grad_sel.astype(jnp.float32))
    return part_q, part_k, part_v


def reference(queries, keys, values, grad_out, offsets):
    shape_heads = (TOKENS, HEADS, HEAD_DIM)
    query_heads = queries.reshape(shape_heads)
    key_heads = keys.reshape(shape_heads)
    value_heads = values.reshape(shape_heads)
    grad_heads = grad_out.reshape(shape_heads)
    combined = jnp.full((TOKENS, HEADS), -jnp.inf, jnp.float32)
    for level in range(LEVELS):
        dilation, per_segment, groups = level_plan(level)
        rows, heads = dilated_index(level, offsets, dilation)
        query_sel = query_heads[rows, heads].reshape(groups, per_segment, HEADS, HEAD_DIM)
        key_sel = key_heads[rows, heads].reshape(groups, per_segment, HEADS, HEAD_DIM)
        level_lse = lax.map(segment_lse, (query_sel, key_sel)).reshape(-1, HEADS)
        combined = combined.at[rows, heads].set(jnp.logaddexp(combined[rows, heads], level_lse))
    output = jnp.zeros(shape_heads, jnp.float32)
    for level in range(LEVELS):
        dilation, per_segment, groups = level_plan(level)
        rows, heads = dilated_index(level, offsets, dilation)
        seg_shape = (groups, per_segment, HEADS, HEAD_DIM)
        items = (query_heads[rows, heads].reshape(seg_shape), key_heads[rows, heads].reshape(seg_shape),
                 value_heads[rows, heads].reshape(seg_shape), combined[rows, heads].reshape(groups, per_segment, HEADS))
        part = lax.map(segment_output, items).reshape(-1, HEADS, HEAD_DIM)
        output = output.at[rows, heads].add(part)
    delta = jnp.sum(grad_heads.astype(jnp.float32) * output, axis=-1)
    grad_q = jnp.zeros(shape_heads, jnp.float32)
    grad_k = jnp.zeros(shape_heads, jnp.float32)
    grad_v = jnp.zeros(shape_heads, jnp.float32)
    for level in range(LEVELS):
        dilation, per_segment, groups = level_plan(level)
        rows, heads = dilated_index(level, offsets, dilation)
        seg_shape = (groups, per_segment, HEADS, HEAD_DIM)
        stat_shape = (groups, per_segment, HEADS)
        items = (query_heads[rows, heads].reshape(seg_shape), key_heads[rows, heads].reshape(seg_shape),
                 value_heads[rows, heads].reshape(seg_shape), grad_heads[rows, heads].reshape(seg_shape),
                 combined[rows, heads].reshape(stat_shape), delta[rows, heads].reshape(stat_shape))
        part_q, part_k, part_v = lax.map(segment_grads, items)
        grad_q = grad_q.at[rows, heads].add(part_q.reshape(-1, HEADS, HEAD_DIM))
        grad_k = grad_k.at[rows, heads].add(part_k.reshape(-1, HEADS, HEAD_DIM))
        grad_v = grad_v.at[rows, heads].add(part_v.reshape(-1, HEADS, HEAD_DIM))
    width = HEADS * HEAD_DIM
    return (grad_q.reshape(TOKENS, width).astype(jnp.bfloat16), grad_k.reshape(TOKENS, width).astype(jnp.bfloat16),
            grad_v.reshape(TOKENS, width).astype(jnp.bfloat16))
```

```python
import math

import jax
import jax.numpy as jnp
from jax import lax
from jax.experimental import pallas as pl
from jax.experimental.pallas import tpu as pltpu
from jax.sharding import PartitionSpec as P

HEADS = 8
HEAD_DIM = 64
KEYS = 1024
ROWS = 128
HALF = ROWS // 2
GROUP = 8
SEGMENTS = 32
WIDE = 512
FEW = 32
PAIR = 2 * HEAD_DIM
SCALE = HEAD_DIM ** (-0.5)
TO_EXP2 = SCALE * math.log2(math.e)
LOWEST = -1e30
MESH = pl.DeviceIdType.MESH
F32 = jnp.float32
BF16 = jnp.bfloat16
COLS = 256
DEEP = 128


def dot(x, y):
    return jnp.dot(x, y, preferred_element_type=F32)


def dot_nt(x, y):
    return lax.dot_general(x, y, (((1,), (1,)), ((), ())), preferred_element_type=F32)


def iota(shape, dim):
    return lax.broadcasted_iota(jnp.int32, shape, dim)


def two_parts(x):
    high = x.astype(BF16)
    return high, (x - high.astype(F32)).astype(BF16)


def fold8(x, op):
    parts = [x[8 * i : 8 * i + 8] for i in range(x.shape[0] // 8)]
    while len(parts) > 1:
        parts = [op(parts[i], parts[i + 1]) for i in range(0, len(parts), 2)]
    return parts[0]


def kernel(
    off_ref,
    q_ref,
    k_ref,
    v_ref,
    g_ref,
    oq_ref,
    ok_ref,
    ov_ref,
    send,
    gath,
    peer,
    keys2,
    part1,
    part2,
    got1,
    got2,
    outkv,
    outq,
    finkv,
    finq,
    score0,
    dprob0,
    score1,
    dprob1,
    dsc0,
    dsc1,
    acc,
    in_send,
    in_recv,
    own_sem,
    l1_send,
    l1_recv,
    l2_send,
    l2_recv,
    b1_send,
    b1_recv,
    b2_send,
    b2_recv,
    kv_send,
    kv_recv,
    dq_send,
    dq_recv,
    home_sem,
):
    major = lax.axis_index("ctxa")
    minor = lax.axis_index("ctxb")
    seg = major * 4 + minor // GROUP
    head = minor % GROUP

    def at_head(other):
        return (major, (minor // GROUP) * GROUP + other)

    def at_seg(other):
        return (other // 4, (other % 4) * GROUP + head)

    partner = seg + 1 - 2 * (seg % 2)

    barrier = pltpu.get_barrier_semaphore()
    for r in range(1, GROUP):
        pl.semaphore_signal(
            barrier, inc=1, device_id=at_head((head + r) % GROUP), device_id_type=MESH
        )

    def greet(r, carry):
        pl.semaphore_signal(
            barrier, inc=1, device_id=at_seg((seg + r) % SEGMENTS), device_id_type=MESH
        )
        return carry

    lax.fori_loop(1, SEGMENTS, greet, 0)

    row = iota((ROWS, ROWS), 0)
    col = iota((ROWS, ROWS), 1)
    split = (col == jnp.where(row < HALF, 2 * row, 2 * row - (ROWS - 1))).astype(F32).astype(BF16)
    low = iota((ROWS, PAIR), 1) < HEAD_DIM
    low_half = iota((HALF, PAIR), 1) < HEAD_DIM

    for which, (x_ref, y_ref) in enumerate(((k_ref, v_ref), (q_ref, g_ref))):
        x_all = dot(split, x_ref[...])
        y_all = dot(split, y_ref[...])
        for t in range(HEADS // 2):
            x = x_all[:, t * PAIR : (t + 1) * PAIR]
            y = y_all[:, t * PAIR : (t + 1) * PAIR]
            for h, both in (
                (2 * t, jnp.where(low, x, pltpu.roll(y, HEAD_DIM, 1))),
                (2 * t + 1, jnp.where(low, pltpu.roll(x, HEAD_DIM, 1), y)),
            ):
                even = off_ref[1, h] == 0
                send[h, which, 0] = jnp.where(even, both[:HALF], both[HALF:]).astype(BF16)
                send[h, which, 1] = jnp.where(even, both[HALF:], both[:HALF]).astype(BF16)

    pl.semaphore_wait(barrier, GROUP - 1 + SEGMENTS - 1)

    mine = pl.ds(pl.multiple_of(head * HALF, HALF), HALF)
    inward = []
    for r in range(1, GROUP):
        other = (head + r) % GROUP
        copy = pltpu.make_async_remote_copy(
            src_ref=send.at[other],
            dst_ref=gath.at[:, :, mine, :],
            send_sem=in_send.at[r],
            recv_sem=in_recv.at[r],
            device_id=at_head(other),
            device_id_type=MESH,
        )
        copy.start()
        inward.append(copy)
    own = pltpu.make_async_copy(send.at[head], gath.at[:, :, mine, :], own_sem)
    own.start()
    own.wait()
    for copy in inward:
        copy.wait_recv()

    level1 = pltpu.make_async_remote_copy(
        src_ref=gath.at[0, 0],
        dst_ref=peer,
        send_sem=l1_send,
        recv_sem=l1_recv,
        device_id=at_seg(partner),
        device_id_type=MESH,
    )
    level1.start()

    off1 = off_ref[1, head]
    off2 = off_ref[2, head]
    base = jnp.where((off1 + off2) % 2 == 0, 0, WIDE) + (off2 >> 1)
    few = iota((FEW, KEYS), 0)
    pick = iota((FEW, KEYS), 1) == base + (few >> 2) * HALF + (few & 3) * 16
    few_t = iota((KEYS, FEW), 1)
    pick_t = iota((KEYS, FEW), 0) == base + (few_t >> 2) * HALF + (few_t & 3) * 16
    pick_low = pick.astype(F32).astype(BF16)
    pick_t_low = pick_t.astype(F32).astype(BF16)

    kv = gath[0].reshape(KEYS, PAIR)
    qg = gath[1].reshape(KEYS, PAIR)
    here = pl.ds(pl.multiple_of(seg * FEW, FEW), FEW)
    keys2[here, :] = dot(pick_low, kv).astype(BF16)

    def level2_copy(r):
        return pltpu.make_async_remote_copy(
            src_ref=keys2.at[here, :],
            dst_ref=keys2.at[here, :],
            send_sem=l2_send.at[r],
            recv_sem=l2_recv.at[r],
            device_id=at_seg((seg + r) % SEGMENTS),
            device_id_type=MESH,
        )

    def level2_start(r, carry):
        level2_copy(r).start()
        return carry

    lax.fori_loop(1, SEGMENTS, level2_start, 0)

    lane_low = iota((1, PAIR), 1) < HEAD_DIM
    zero = jnp.zeros((), BF16)
    kv_k = jnp.where(lane_low, kv, zero)
    kv_v = jnp.where(lane_low, zero, kv)
    qg_q = jnp.where(lane_low, qg * jnp.asarray(SCALE, BF16), zero)
    qg_g = jnp.where(lane_low, zero, qg)
    qg_t = qg.T
    kv_t = kv.T

    def stats(k_rows, v_rows, columns, score, dprob, weights):
        across = qg_t[:, columns]
        depth = k_rows.shape[0]
        high8 = jnp.full((8, COLS), LOWEST, F32)
        for j in range(0, depth, DEEP):
            s = dot(k_rows[j : j + DEEP], across) * TO_EXP2
            score[j : j + DEEP, columns] = s
            high8 = jnp.maximum(high8, fold8(s, jnp.maximum))
        high = jnp.max(high8, axis=0, keepdims=True)
        sum8 = jnp.zeros((8, COLS), F32)
        dot8 = jnp.zeros((8, COLS), F32)
        for j, weight in zip(range(0, depth, DEEP), weights):
            e = jnp.exp2(score[j : j + DEEP, columns] - high)
            score[j : j + DEEP, columns] = e
            d = dot(v_rows[j : j + DEEP], across)
            dprob[j : j + DEEP, columns] = d
            sum8 = sum8 + weight * fold8(e, jnp.add)
            dot8 = dot8 + weight * fold8(e * d, jnp.add)
        return (
            high,
            jnp.sum(sum8, axis=0, keepdims=True),
            jnp.sum(dot8, axis=0, keepdims=True),
        )

    def joined(items):
        return [jnp.concatenate([item[i] for item in items], axis=1) for i in range(3)]

    blocks0 = []
    for c in range(0, KEYS, COLS):
        twice = 2.0 if c < WIDE else 1.0
        weights = [twice if j < WIDE else 1.0 for j in range(0, KEYS, DEEP)]
        blocks0.append(stats(kv_k, kv_v, slice(c, c + COLS), score0, dprob0, weights))
    high0, sum0, dot0 = joined(blocks0)

    level1.wait_recv()
    kv1 = peer[...]
    kv1_k = jnp.where(lane_low, kv1, zero)
    kv1_v = jnp.where(lane_low, zero, kv1)
    blocks1 = []
    for c in range(0, WIDE, COLS):
        weights = [1.0] * (WIDE // DEEP)
        blocks1.append(stats(kv1_k, kv1_v, slice(c, c + COLS), score1, dprob1, weights))
    blocks1.append(
        (jnp.full((1, WIDE), LOWEST, F32), jnp.zeros((1, WIDE), F32), jnp.zeros((1, WIDE), F32))
    )
    high1, sum1, dot1 = joined(blocks1)

    def level2_wait(r, carry):
        level2_copy(r).wait_recv()
        return carry

    lax.fori_loop(1, SEGMENTS, level2_wait, 0)
    kv2 = keys2[...]
    qg2 = dot(pick_low, qg)
    few_low = iota((FEW, PAIR), 1) < HEAD_DIM
    qg2_q = jnp.where(few_low, qg2, 0.0).astype(BF16)
    qg2_g = jnp.where(few_low, 0.0, qg2).astype(BF16)
    s2 = dot_nt(qg2_q, kv2) * TO_EXP2
    d2 = dot_nt(qg2_g, kv2)
    high2 = jnp.max(s2, axis=1, keepdims=True)
    e2 = jnp.exp2(s2 - high2)
    sum2 = jnp.sum(e2, axis=1, keepdims=True)
    dot2 = jnp.sum(e2 * d2, axis=1, keepdims=True)

    def spread(x, filler):
        return jnp.where(pick, x, filler)

    high2_row = jnp.max(spread(high2, LOWEST), axis=0, keepdims=True)
    sum2_row = jnp.sum(spread(sum2, 0.0), axis=0, keepdims=True)
    dot2_row = jnp.sum(spread(dot2, 0.0), axis=0, keepdims=True)

    top = jnp.maximum(jnp.maximum(high0, high1), high2_row)
    w0 = jnp.exp2(high0 - top)
    w1 = jnp.exp2(high1 - top)
    w2_row = jnp.exp2(high2_row - top)
    inverse = 1.0 / (w0 * sum0 + w1 * sum1 + w2_row * sum2_row)
    delta = (w0 * dot0 + w1 * dot1 + w2_row * dot2_row) * inverse
    w0 = w0 * inverse
    w1 = w1 * inverse
    w2 = jnp.sum(spread(w2_row * inverse, 0.0), axis=1, keepdims=True)
    delta2 = jnp.sum(spread(delta, 0.0), axis=1, keepdims=True)

    p2 = e2 * w2
    ds2 = p2 * (d2 - delta2)
    scaled_q2 = (qg2_q * jnp.asarray(SCALE, BF16)).astype(BF16)
    kv_grad2 = dot(ds2.T.astype(BF16), scaled_q2) + dot(p2.T.astype(BF16), qg2_g)
    part2[...] = kv_grad2.astype(BF16)

    def back2_copy(r):
        other = (seg + r) % SEGMENTS
        return pltpu.make_async_remote_copy(
            src_ref=part2.at[pl.ds(pl.multiple_of(other * FEW, FEW), FEW), :],
            dst_ref=got2.at[r],
            send_sem=b2_send.at[r],
            recv_sem=b2_recv.at[r],
            device_id=at_seg(other),
            device_id_type=MESH,
        )

    def back2_start(r, carry):
        back2_copy(r).start()
        return carry

    lax.fori_loop(1, SEGMENTS, back2_start, 0)
    dq2 = dot(ds2.astype(BF16), kv2)

    def grads(depth, width, score, dprob, dsc, weight_of, out):
        for j in range(0, depth, DEEP):
            total = jnp.zeros((DEEP, PAIR), F32)
            for c in range(0, width, COLS):
                columns = slice(c, c + COLS)
                p = score[j : j + DEEP, columns] * weight_of(j, c)
                ds = (p * (dprob[j : j + DEEP, columns] - delta[:, columns])).astype(BF16)
                dsc[j : j + DEEP, columns] = ds
                total = total + dot(ds, qg_q[columns]) + dot(p.astype(BF16), qg_g[columns])
            out(j, total)

    def store1(j, total):
        part1[j : j + DEEP] = total.astype(BF16)

    grads(WIDE, WIDE, score1, dprob1, dsc1, lambda j, c: w1[:, c : c + COLS], store1)
    back1 = pltpu.make_async_remote_copy(
        src_ref=part1,
        dst_ref=got1,
        send_sem=b1_send,
        recv_sem=b1_recv,
        device_id=at_seg(partner),
        device_id_type=MESH,
    )
    back1.start()

    def store0(j, total):
        acc[j : j + DEEP] = total

    def weight0(j, c):
        w = w0[:, c : c + COLS]
        return 2.0 * w if j < WIDE and c < WIDE else w

    grads(KEYS, KEYS, score0, dprob0, dsc0, weight0, store0)

    k_t = kv_t[:HEAD_DIM]
    k1_t = kv1.T[:HEAD_DIM]
    high, rest = two_parts(dq2.T[:HEAD_DIM])
    halves = []
    for half in range(2):
        columns = slice(half * WIDE, (half + 1) * WIDE)
        total = dot(k_t, dsc0[:, columns])
        if half == 0:
            total = total + dot(k1_t, dsc1[...])
        total = total + dot(high, pick_low[:, columns]) + dot(rest, pick_low[:, columns])
        halves.append(total)
    dq_t = jnp.concatenate(halves, axis=0) * SCALE
    outq[...] = dq_t.T.astype(BF16)

    outward = []
    for r in range(1, GROUP):
        other = (head + r) % GROUP
        theirs = pl.ds(pl.multiple_of(other * HALF, HALF), HALF)
        copy = pltpu.make_async_remote_copy(
            src_ref=outq.at[theirs, :],
            dst_ref=finq.at[head],
            send_sem=dq_send.at[r],
            recv_sem=dq_recv.at[r],
            device_id=at_head(other),
            device_id_type=MESH,
        )
        copy.start()
        outward.append(copy)
    home_q = pltpu.make_async_copy(outq.at[mine, :], finq.at[head], home_sem.at[0])
    home_q.start()

    def back2_wait(r, total):
        back2_copy(r).wait_recv()
        return total + got2[r].astype(F32)

    own2 = part2[here, :].astype(F32)
    sum_few = lax.fori_loop(1, SEGMENTS, back2_wait, own2)
    high, rest = two_parts(sum_few)
    added = dot(pick_t_low, high) + dot(pick_t_low, rest)
    back1.wait_recv()
    outkv[0] = (acc[:WIDE] + added[:WIDE] + got1[...].astype(F32)).astype(BF16)
    outkv[1] = (acc[WIDE:] + added[WIDE:]).astype(BF16)
    for r in range(1, GROUP):
        other = (head + r) % GROUP
        theirs = pl.ds(pl.multiple_of(other * HALF, HALF), HALF)
        copy = pltpu.make_async_remote_copy(
            src_ref=outkv.at[:, theirs, :],
            dst_ref=finkv.at[head],
            send_sem=kv_send.at[r],
            recv_sem=kv_recv.at[r],
            device_id=at_head(other),
            device_id_type=MESH,
        )
        copy.start()
        outward.append(copy)
    home_kv = pltpu.make_async_copy(outkv.at[:, mine, :], finkv.at[head], home_sem.at[1])
    home_kv.start()

    for copy in inward:
        copy.wait_send()
    level1.wait_send()
    back1.wait_send()

    def sent2(r, carry):
        level2_copy(r).wait_send()
        back2_copy(r).wait_send()
        return carry

    lax.fori_loop(1, SEGMENTS, sent2, 0)

    home_q.wait()
    home_kv.wait()
    for copy in outward:
        copy.wait()

    merge = (row == jnp.where(col < HALF, 2 * col, 2 * col - (ROWS - 1))).astype(F32).astype(BF16)

    def ordered(h):
        even = off_ref[1, h] == 0
        first = finkv[h, 0].astype(F32)
        second = finkv[h, 1].astype(F32)
        return jnp.concatenate(
            [jnp.where(even, first, second), jnp.where(even, second, first)], axis=0
        )

    for t in range(HEADS // 2):
        lanes = slice(t * PAIR, (t + 1) * PAIR)
        a = ordered(2 * t)
        b = ordered(2 * t + 1)
        dk = jnp.where(low, a, pltpu.roll(b, HEAD_DIM, 1)).astype(BF16)
        dv = jnp.where(low, pltpu.roll(a, HEAD_DIM, 1), b).astype(BF16)
        ok_ref[:, lanes] = dot(merge, dk).astype(BF16)
        ov_ref[:, lanes] = dot(merge, dv).astype(BF16)
        xa = finq[2 * t].astype(F32)
        xb = finq[2 * t + 1].astype(F32)
        ra = pltpu.roll(xa, HEAD_DIM, 1)
        rb = pltpu.roll(xb, HEAD_DIM, 1)
        even_a = off_ref[1, 2 * t] == 0
        even_b = off_ref[1, 2 * t + 1] == 0
        evens = jnp.where(low_half, jnp.where(even_a, xa, ra), jnp.where(even_b, rb, xb))
        odds = jnp.where(low_half, jnp.where(even_a, ra, xa), jnp.where(even_b, xb, rb))
        dq = jnp.concatenate([evens, odds], axis=0).astype(BF16)
        oq_ref[:, lanes] = dot(merge, dq).astype(BF16)


def local(queries, keys, values, grad_out, offsets):
    vmem = pl.BlockSpec(memory_space=pltpu.VMEM)
    shape = jax.ShapeDtypeStruct((ROWS, HEADS * HEAD_DIM), BF16)
    dma = pltpu.SemaphoreType.DMA
    return pl.pallas_call(
        kernel,
        out_shape=(shape, shape, shape),
        in_specs=[pl.BlockSpec(memory_space=pltpu.SMEM), vmem, vmem, vmem, vmem],
        out_specs=(vmem, vmem, vmem),
        scratch_shapes=[
            pltpu.VMEM((HEADS, 2, 2, HALF, PAIR), BF16),
            pltpu.VMEM((2, 2, WIDE, PAIR), BF16),
            pltpu.VMEM((WIDE, PAIR), BF16),
            pltpu.VMEM((KEYS, PAIR), BF16),
            pltpu.VMEM((WIDE, PAIR), BF16),
            pltpu.VMEM((KEYS, PAIR), BF16),
            pltpu.VMEM((WIDE, PAIR), BF16),
            pltpu.VMEM((SEGMENTS, FEW, PAIR), BF16),
            pltpu.VMEM((2, WIDE, PAIR), BF16),
            pltpu.VMEM((WIDE, PAIR), BF16),
            pltpu.VMEM((HEADS, 2, HALF, PAIR), BF16),
            pltpu.VMEM((HEADS, HALF, PAIR), BF16),
            pltpu.VMEM((KEYS, KEYS), F32),
            pltpu.VMEM((KEYS, KEYS), F32),
            pltpu.VMEM((WIDE, WIDE), F32),
            pltpu.VMEM((WIDE, WIDE), F32),
            pltpu.VMEM((KEYS, KEYS), BF16),
            pltpu.VMEM((WIDE, WIDE), BF16),
            pltpu.VMEM((KEYS, PAIR), F32),
            dma((GROUP,)),
            dma((GROUP,)),
            dma,
            dma,
            dma,
            dma((SEGMENTS,)),
            dma((SEGMENTS,)),
            dma,
            dma,
            dma((SEGMENTS,)),
            dma((SEGMENTS,)),
            dma((GROUP,)),
            dma((GROUP,)),
            dma((GROUP,)),
            dma((GROUP,)),
            dma((2,)),
        ],
        compiler_params=pltpu.CompilerParams(
            collective_id=0, has_side_effects=True, vmem_limit_bytes=50 * 1024 * 1024
        ),
    )(offsets, queries, keys, values, grad_out)


def solution(mesh):
    rows = P(("ctxa", "ctxb"), None)
    return jax.shard_map(
        local,
        mesh=mesh,
        in_specs=(rows, rows, rows, rows, P()),
        out_specs=(rows, rows, rows),
        check_vma=False,
    )
```

```python
import math

import jax
import jax.numpy as jnp
from jax import lax
from jax.experimental import pallas as pl
from jax.experimental.pallas import tpu as pltpu
from jax.sharding import PartitionSpec as P

HEADS = 8
HEAD_DIM = 64
KEYS = 1024
LEVELS = 3
ROWS = 128
HALF = ROWS // 2
GROUP = 8
MATES = 16
WIDE = 512
FEW = 32
TILE = 16
QUARTER = HALF // 2
PAIR = 2 * HEAD_DIM
SCALE = HEAD_DIM ** (-0.5)
TO_EXP2 = SCALE * math.log2(math.e)
LOWEST = -1e30
MESH = pl.DeviceIdType.MESH
F32 = jnp.float32
BF16 = jnp.bfloat16
COLS = 256
SLOTS = COLS // HALF
DEEP = 128


def dot(x, y):
    return jnp.dot(x, y, preferred_element_type=F32)


def dot_nt(x, y):
    return lax.dot_general(x, y, (((1,), (1,)), ((), ())), preferred_element_type=F32)


def iota(shape, dim):
    return lax.broadcasted_iota(jnp.int32, shape, dim)


def one_hot(hit):
    return hit.astype(F32).astype(BF16)


def two_parts(x):
    high = x.astype(BF16)
    return high, (x - high.astype(F32)).astype(BF16)


def fold8(x, op):
    parts = [x[8 * i : 8 * i + 8] for i in range(x.shape[0] // 8)]
    while len(parts) > 1:
        parts = [op(parts[i], parts[i + 1]) for i in range(0, len(parts), 2)]
    return parts[0]


def kernel(
    off_hbm,
    q_hbm,
    k_hbm,
    v_hbm,
    g_hbm,
    out_ref,
    off_ref,
    q_ref,
    k_ref,
    v_ref,
    g_ref,
    send_few,
    send_kv,
    send_qg,
    few,
    kv,
    qg,
    peer,
    keys2,
    kv_k,
    kv_v,
    k_t,
    part1,
    got1,
    part2,
    part2_own,
    sib,
    back2,
    got2,
    out_kv,
    out_q,
    fin_kv,
    fin_q,
    score,
    dprob,
    dsc,
    acc,
    few_sem,
    kv_sem,
    qg_sem,
    l1_sem,
    l2_sem,
    pass_sem,
    b1_sem,
    half_sem,
    b2_sem,
    dq_sem,
    home_sem,
    load_sem,
):
    loads = []
    for i, (src, dst) in enumerate(
        ((k_hbm, k_ref), (v_hbm, v_ref), (q_hbm, q_ref), (g_hbm, g_ref), (off_hbm, off_ref))
    ):
        load = pltpu.make_async_copy(src, dst, load_sem.at[i])
        load.start()
        loads.append(load)

    major = lax.axis_index("ctxa")
    minor = lax.axis_index("ctxb")
    head = minor % GROUP
    mate = (major // 2) * 4 + minor // GROUP

    def member(dx, dy):
        x = (head % 4 + dx) % 4
        y = (head // 4 + dy) % 2
        return y * 4 + x

    def at_head(other):
        return (major, (minor // GROUP) * GROUP + other)

    def at_mate(other):
        return ((other // 4) * 2 + major % 2, (other % 4) * GROUP + head)

    ahead = [member(r % 4, r // 4) for r in range(GROUP)]
    behind = [member(4 - r % 4, r // 4) for r in range(GROUP)]
    sibling = (major + 1 - 2 * (major % 2), minor)
    partner = (major, minor + GROUP - 2 * GROUP * ((minor // GROUP) % 2))

    def remote(src, dst, sems, device):
        return pltpu.make_async_remote_copy(
            src_ref=src,
            dst_ref=dst,
            send_sem=sems[0],
            recv_sem=sems[1],
            device_id=device,
            device_id_type=MESH,
        )

    def pair_of(sem, *index):
        return (sem.at[(0, *index)], sem.at[(1, *index)])

    barrier = pltpu.get_barrier_semaphore()

    def greet(device):
        pl.semaphore_signal(barrier, inc=1, device_id=device, device_id_type=MESH)

    for r in range(1, GROUP):
        greet(at_head(ahead[r]))
    for r in range(1, MATES):
        greet(at_mate((mate + r) % MATES))
    greet(sibling)

    row = iota((ROWS, ROWS), 0)
    col = iota((ROWS, ROWS), 1)
    split = one_hot(col == jnp.where(row < HALF, 2 * row, 2 * row - (ROWS - 1)))
    low = iota((ROWS, PAIR), 1) < HEAD_DIM

    for load in loads:
        load.wait()
    order = [[None, None] for _ in range(HEADS)]
    for which, (x_ref, y_ref, packed) in enumerate(
        ((k_ref, v_ref, send_kv), (q_ref, g_ref, send_qg))
    ):
        x_all = dot(split, x_ref[...])
        y_all = dot(split, y_ref[...])
        for t in range(HEADS // 2):
            x = x_all[:, t * PAIR : (t + 1) * PAIR]
            y = y_all[:, t * PAIR : (t + 1) * PAIR]
            for h, both in (
                (2 * t, jnp.where(low, x, pltpu.roll(y, HEAD_DIM, 1))),
                (2 * t + 1, jnp.where(low, pltpu.roll(x, HEAD_DIM, 1), y)),
            ):
                even = off_ref[1, h] == 0
                first = jnp.where(even, both[:HALF], both[HALF:]).astype(BF16)
                second = jnp.where(even, both[HALF:], both[:HALF]).astype(BF16)
                packed[h, 0] = first
                packed[h, 1] = second
                order[h][which] = [first, second]
    tile_row = iota((TILE, 2 * ROWS), 0)
    tile_col = iota((TILE, 2 * ROWS), 1)
    wanted = (tile_row >> 2) * ROWS + (tile_row & 3) * 16
    for h in range(HEADS):
        place = ((off_ref[1, h] + off_ref[2, h]) % 2) * HALF + (off_ref[2, h] >> 1)
        hit = one_hot((tile_col == wanted + place) & (tile_row < 8))
        send_few[h] = dot(hit, jnp.concatenate(order[h][0] + order[h][1], axis=0)).astype(BF16)

    pl.semaphore_wait(barrier, GROUP - 1 + MATES - 1 + 1)

    in_few, in_kv, in_qg = [], [], [[], []]
    for r in range(1, GROUP):
        other = ahead[r]
        tile = pl.ds(r * TILE, TILE)
        in_few.append(
            remote(send_few.at[other], few.at[tile, :], pair_of(few_sem, r), at_head(other))
        )
        in_few[-1].start()
    for r in range(1, GROUP):
        other = ahead[r]
        slot = pl.ds(r * HALF, HALF)
        in_kv.append(
            remote(send_kv.at[other], kv.at[:, slot, :], pair_of(kv_sem, r), at_head(other))
        )
        in_kv[-1].start()
    for half in range(2):
        for r in range(1, GROUP):
            other = ahead[r]
            slot = pl.ds(r * HALF, HALF)
            in_qg[half].append(
                remote(
                    send_qg.at[other, half],
                    qg.at[half, slot, :],
                    pair_of(qg_sem, half, r),
                    at_head(other),
                )
            )
            in_qg[half][-1].start()
    few[:TILE] = send_few[head]
    kv[:, :HALF] = send_kv[head]
    qg[:, :HALF] = send_qg[head]

    off1 = off_ref[1, head]
    off2 = off_ref[2, head]
    inside = (off1 + off2) % 2 == 0
    base = jnp.where(inside, 0, WIDE) + (off2 >> 1)
    at = iota((FEW, KEYS), 0)
    pick = iota((FEW, KEYS), 1) == base + (at >> 2) * HALF + (at & 3) * 16
    at = iota((KEYS, FEW), 1)
    pick_t = one_hot(iota((KEYS, FEW), 0) == base + (at >> 2) * HALF + (at & 3) * 16)
    pick_low = one_hot(pick)
    at = iota((2 * FEW, GROUP * TILE), 0)
    gather = one_hot(
        iota((2 * FEW, GROUP * TILE), 1)
        == ((at % FEW) >> 2) * TILE + (at & 3) + jnp.where(at < FEW, 0, 4)
    )
    for copy in in_few:
        copy.wait_recv()
    picked = dot(gather, few[...])
    keys2[0, mate] = picked[:FEW].astype(BF16)
    qg2 = picked[FEW:]

    def level2(r):
        block = keys2.at[0, mate]
        return remote(block, block, pair_of(l2_sem, r), at_mate((mate + r) % MATES))

    def level2_start(r, carry):
        level2(r).start()
        return carry

    lax.fori_loop(1, MATES, level2_start, 0)

    level1 = []
    for r in range(GROUP):
        if r:
            in_kv[r - 1].wait_recv()
        slot = pl.ds(r * HALF, HALF)
        level1.append(remote(kv.at[0, slot, :], peer.at[slot, :], pair_of(l1_sem, r), partner))
        level1[-1].start()

    lane_low = iota((1, PAIR), 1) < HEAD_DIM
    zero = jnp.zeros((), BF16)
    kv_all = kv[...].reshape(KEYS, PAIR)
    kv_k[:KEYS] = jnp.where(lane_low, kv_all, zero)
    kv_v[:KEYS] = jnp.where(lane_low, zero, kv_all)
    k_t[:, :KEYS] = kv_all.T[:HEAD_DIM]

    def level2_wait(r, carry):
        level2(r).wait_recv()
        return carry

    lax.fori_loop(1, MATES, level2_wait, 0)
    passed = remote(keys2.at[0], keys2.at[1], pair_of(pass_sem), sibling)
    passed.start()

    for copy in level1:
        copy.wait_recv()
    peer_all = peer[...]
    kv_k[KEYS:] = jnp.where(lane_low, peer_all, zero)
    kv_v[KEYS:] = jnp.where(lane_low, zero, peer_all)
    k_t[:, KEYS:] = peer_all.T[:HEAD_DIM]
    passed.wait_recv()

    few_low = iota((FEW, PAIR), 1) < HEAD_DIM
    q2 = jnp.where(few_low, qg2, 0.0).astype(BF16)
    g2 = jnp.where(few_low, 0.0, qg2).astype(BF16)
    both2 = jnp.concatenate([q2, g2], axis=0)
    kv2 = keys2[...].reshape(KEYS, PAIR)
    here = dot_nt(both2, kv_all)
    near = dot_nt(both2, peer_all)
    far = dot_nt(both2, kv2)
    s_here = here[:FEW] * TO_EXP2
    s_near = jnp.where(inside, near[:FEW] * TO_EXP2, LOWEST)
    s_far = far[:FEW] * TO_EXP2
    high2 = jnp.maximum(
        jnp.maximum(
            jnp.max(s_here, axis=1, keepdims=True), jnp.max(s_near, axis=1, keepdims=True)
        ),
        jnp.max(s_far, axis=1, keepdims=True),
    )
    twice = jnp.where((iota((FEW, KEYS), 1) < WIDE) & inside, 2.0, 1.0)
    e_here = jnp.exp2(s_here - high2) * twice
    e_near = jnp.exp2(s_near - high2)
    e_far = jnp.exp2(s_far - high2)
    sum2 = jnp.sum(e_far, axis=1, keepdims=True)
    dot2 = jnp.sum(e_far * far[FEW:], axis=1, keepdims=True)
    sum2_all = (
        sum2 + jnp.sum(e_here, axis=1, keepdims=True) + jnp.sum(e_near, axis=1, keepdims=True)
    )
    dot2_all = (
        dot2
        + jnp.sum(e_here * here[FEW:], axis=1, keepdims=True)
        + jnp.sum(e_near * near[FEW:], axis=1, keepdims=True)
    )
    inverse2 = 1.0 / sum2_all
    p2 = e_far * inverse2
    ds2 = p2 * (far[FEW:] - dot2_all * inverse2)
    scaled_q2 = (q2 * jnp.asarray(SCALE, BF16)).astype(BF16)
    kv_grad2 = dot(ds2.T.astype(BF16), scaled_q2) + dot(p2.T.astype(BF16), g2)
    part2[...] = kv_grad2[WIDE:].astype(BF16)
    halved = remote(part2, sib, pair_of(half_sem), sibling)
    halved.start()
    part2_own[...] = kv_grad2[:WIDE]
    dq2_parts = two_parts(dot(ds2.astype(BF16), kv2).T[:HEAD_DIM])
    high2_row = jnp.max(jnp.where(pick, high2, LOWEST), axis=0, keepdims=True)
    sum2_row = jnp.sum(jnp.where(pick, sum2, 0.0), axis=0, keepdims=True)
    dot2_row = jnp.sum(jnp.where(pick, dot2, 0.0), axis=0, keepdims=True)

    out_copies = []

    def block(c):
        half = c // 2
        first = (c % 2) * COLS
        columns = slice(c * COLS, (c + 1) * COLS)
        for r in range(max(1, first // HALF), first // HALF + SLOTS):
            in_qg[half][r - 1].wait_recv()
        mine = qg[half, first : first + COLS, :]
        across = mine.T
        scaled_q = jnp.where(lane_low, mine * jnp.asarray(SCALE, BF16), zero)
        only_g = jnp.where(lane_low, zero, mine)
        depth = KEYS + WIDE if half == 0 else KEYS
        steps = range(0, depth, DEEP)
        high8 = jnp.full((8, COLS), LOWEST, F32)
        for j in steps:
            s = dot(kv_k[j : j + DEEP], across) * TO_EXP2
            score[j : j + DEEP] = s
            high8 = jnp.maximum(high8, fold8(s, jnp.maximum))
        high = jnp.maximum(jnp.max(high8, axis=0, keepdims=True), high2_row[:, columns])
        sum8 = jnp.zeros((8, COLS), F32)
        dot8 = jnp.zeros((8, COLS), F32)

        def weight(j):
            return 2.0 if half == 0 and j < WIDE else 1.0

        for j in steps:
            e = jnp.exp2(score[j : j + DEEP] - high)
            score[j : j + DEEP] = e
            d = dot(kv_v[j : j + DEEP], across)
            dprob[j : j + DEEP] = d
            sum8 = sum8 + weight(j) * fold8(e, jnp.add)
            dot8 = dot8 + weight(j) * fold8(e * d, jnp.add)
        shift2 = jnp.exp2(high2_row[:, columns] - high)
        total = jnp.sum(sum8, axis=0, keepdims=True) + shift2 * sum2_row[:, columns]
        product = jnp.sum(dot8, axis=0, keepdims=True) + shift2 * dot2_row[:, columns]
        inverse = 1.0 / total
        delta = product * inverse
        for j in steps:
            p = score[j : j + DEEP] * (weight(j) * inverse)
            ds = (p * (dprob[j : j + DEEP] - delta)).astype(BF16)
            dsc[j : j + DEEP] = ds
            added = dot(ds, scaled_q) + dot(p.astype(BF16), only_g)
            acc[j : j + DEEP] = added if c == 0 else acc[j : j + DEEP] + added
        dq_t = dot(k_t[:, :depth], dsc[:depth])
        for part in dq2_parts:
            dq_t = dq_t + dot(part, pick_low[:, columns])
        dq = (dq_t * SCALE).T
        lanes = [
            jnp.concatenate([dq[i * HALF + b : i * HALF + b + QUARTER] for i in range(SLOTS)], 0)
            for b in (0, QUARTER)
        ]
        rows = slice((c % 2) * SLOTS * QUARTER, (c % 2 + 1) * SLOTS * QUARTER)
        out_q[half, rows] = jnp.concatenate(lanes, axis=1).astype(BF16)
        for r in range(first // HALF, first // HALF + SLOTS):
            slot = pl.ds(r * QUARTER, QUARTER)
            if r == 0:
                fin_q[half, head] = out_q[half, :QUARTER]
            else:
                copy = remote(
                    out_q.at[half, slot, :],
                    fin_q.at[half, head],
                    pair_of(dq_sem, half, r),
                    at_head(behind[r]),
                )
                copy.start()
                out_copies.append(copy)

    block(0)
    halved.wait_recv()
    back2[...] = (part2_own[...] + sib[...].astype(F32)).astype(BF16)

    def level2_back(r):
        other = (mate + r) % MATES
        return remote(
            back2.at[pl.ds(pl.multiple_of(other * FEW, FEW), FEW), :],
            got2.at[r],
            pair_of(b2_sem, r),
            at_mate(other),
        )

    def level2_back_start(r, carry):
        level2_back(r).start()
        return carry

    lax.fori_loop(1, MATES, level2_back_start, 0)
    block(1)
    part1[...] = acc[KEYS:].astype(BF16)
    back1 = remote(part1, got1, pair_of(b1_sem), partner)
    back1.start()
    block(2)
    block(3)

    def level2_back_wait(r, total):
        level2_back(r).wait_recv()
        return total + got2[r].astype(F32)

    own2 = back2[pl.ds(pl.multiple_of(mate * FEW, FEW), FEW), :].astype(F32)
    sum_few = lax.fori_loop(1, MATES, level2_back_wait, own2)
    upper, lower = two_parts(sum_few)
    added = dot(pick_t, upper) + dot(pick_t, lower)

    def go_home(half):
        for r in range(GROUP):
            slot = pl.ds(r * HALF, HALF)
            if r == 0:
                fin_kv[half, head] = out_kv[half, :HALF]
            else:
                copy = remote(
                    out_kv.at[half, slot, :],
                    fin_kv.at[half, head],
                    pair_of(home_sem, half, r),
                    at_head(behind[r]),
                )
                copy.start()
                out_copies.append(copy)

    out_kv[1] = (acc[WIDE:KEYS] + added[WIDE:]).astype(BF16)
    go_home(1)
    back1.wait_recv()
    out_kv[0] = (acc[:WIDE] + added[:WIDE] + got1[...].astype(F32)).astype(BF16)
    go_home(0)

    for copy in in_few + in_kv + in_qg[0] + in_qg[1] + level1 + [passed, halved, back1]:
        copy.wait_send()

    def sent2(r, carry):
        level2(r).wait_send()
        level2_back(r).wait_send()
        return carry

    lax.fori_loop(1, MATES, sent2, 0)

    for copy in out_copies:
        copy.wait()

    merge = one_hot(row == jnp.where(col < HALF, 2 * col, 2 * col - (ROWS - 1)))
    quarter_low = iota((QUARTER, PAIR), 1) < HEAD_DIM

    def ordered(ref, h):
        even = off_ref[1, h] == 0
        first = ref[0, h].astype(F32)
        second = ref[1, h].astype(F32)
        return jnp.where(even, first, second), jnp.where(even, second, first)

    for t in range(HEADS // 2):
        lanes = slice(t * PAIR, (t + 1) * PAIR)
        a = jnp.concatenate(ordered(fin_kv, 2 * t), axis=0)
        b = jnp.concatenate(ordered(fin_kv, 2 * t + 1), axis=0)
        dk = jnp.where(low, a, pltpu.roll(b, HEAD_DIM, 1)).astype(BF16)
        dv = jnp.where(low, pltpu.roll(a, HEAD_DIM, 1), b).astype(BF16)
        out_ref[1, :, lanes] = dot(merge, dk).astype(BF16)
        out_ref[2, :, lanes] = dot(merge, dv).astype(BF16)
        parts = []
        for a, b in zip(ordered(fin_q, 2 * t), ordered(fin_q, 2 * t + 1)):
            parts.append(jnp.where(quarter_low, a, pltpu.roll(b, HEAD_DIM, 1)))
            parts.append(jnp.where(quarter_low, pltpu.roll(a, HEAD_DIM, 1), b))
        dq = jnp.concatenate(parts, axis=0).astype(BF16)
        out_ref[0, :, lanes] = dot(merge, dq).astype(BF16)


def local(queries, keys, values, grad_out, offsets):
    width = HEADS * HEAD_DIM
    dma = pltpu.SemaphoreType.DMA

    def low_buffer(*shape):
        return pltpu.VMEM(shape, BF16)

    result = pl.pallas_call(
        kernel,
        out_shape=jax.ShapeDtypeStruct((3, ROWS, width), BF16),
        in_specs=[pl.BlockSpec(memory_space=pltpu.HBM)] * 5,
        out_specs=pl.BlockSpec(memory_space=pltpu.VMEM),
        scratch_shapes=[
            pltpu.SMEM((LEVELS, HEADS), jnp.int32),
            low_buffer(ROWS, width),
            low_buffer(ROWS, width),
            low_buffer(ROWS, width),
            low_buffer(ROWS, width),
            low_buffer(HEADS, TILE, PAIR),
            low_buffer(HEADS, 2, HALF, PAIR),
            low_buffer(HEADS, 2, HALF, PAIR),
            low_buffer(GROUP * TILE, PAIR),
            low_buffer(2, WIDE, PAIR),
            low_buffer(2, WIDE, PAIR),
            low_buffer(WIDE, PAIR),
            low_buffer(2, MATES, FEW, PAIR),
            low_buffer(KEYS + WIDE, PAIR),
            low_buffer(KEYS + WIDE, PAIR),
            low_buffer(HEAD_DIM, KEYS + WIDE),
            low_buffer(WIDE, PAIR),
            low_buffer(WIDE, PAIR),
            low_buffer(WIDE, PAIR),
            pltpu.VMEM((WIDE, PAIR), F32),
            low_buffer(WIDE, PAIR),
            low_buffer(WIDE, PAIR),
            low_buffer(MATES, FEW, PAIR),
            low_buffer(2, WIDE, PAIR),
            low_buffer(2, GROUP * QUARTER, PAIR),
            low_buffer(2, HEADS, HALF, PAIR),
            low_buffer(2, HEADS, QUARTER, PAIR),
            pltpu.VMEM((KEYS + WIDE, COLS), F32),
            pltpu.VMEM((KEYS + WIDE, COLS), F32),
            low_buffer(KEYS + WIDE, COLS),
            pltpu.VMEM((KEYS + WIDE, PAIR), F32),
            dma((2, GROUP)),
            dma((2, GROUP)),
            dma((2, 2, GROUP)),
            dma((2, GROUP)),
            dma((2, MATES)),
            dma((2,)),
            dma((2,)),
            dma((2,)),
            dma((2, MATES)),
            dma((2, 2, GROUP)),
            dma((2, 2, GROUP)),
            dma((5,)),
        ],
        compiler_params=pltpu.CompilerParams(
            collective_id=0, has_side_effects=True, vmem_limit_bytes=63 * 1024 * 1024
        ),
    )(offsets, queries, keys, values, grad_out)
    return result[0], result[1], result[2]


def solution(mesh):
    rows = P(("ctxa", "ctxb"), None)
    return jax.shard_map(
        local,
        mesh=mesh,
        in_specs=(rows, rows, rows, rows, P()),
        out_specs=(rows, rows, rows),
        check_vma=False,
    )
```

```python
import math

import jax
import jax.numpy as jnp
from jax import lax
from jax.experimental import pallas as pl
from jax.experimental.pallas import tpu as pltpu
from jax.sharding import PartitionSpec as P

HEADS = 8
HEAD_DIM = 64
KEYS = 1024
LEVELS = 3
ROWS = 128
HALF = ROWS // 2
GROUP = 8
MATES = 16
WIDE = 512
FEW = 32
TILE = 16
QUARTER = HALF // 2
PAIR = 2 * HEAD_DIM
SCALE = HEAD_DIM ** (-0.5)
TO_EXP2 = SCALE * math.log2(math.e)
LOWEST = -1e30
MESH = pl.DeviceIdType.MESH
F32 = jnp.float32
BF16 = jnp.bfloat16
COLS = 256
SLOTS = COLS // HALF
DEEP = 128
FAR_FIRST = (6, 2, 5, 7, 4, 1, 3)
LAYERS = 8
LAYERS_FAR_FIRST = (4, 3, 5, 2, 6, 1, 7)
MATES_FAR_FIRST = (9, 8, 7, 10, 6, 11, 5, 12, 4, 13, 3, 14, 2, 15, 1)


def dot(x, y):
    return jnp.dot(x, y, preferred_element_type=F32)


def dot_nt(x, y):
    return lax.dot_general(x, y, (((1,), (1,)), ((), ())), preferred_element_type=F32)


def iota(shape, dim):
    return lax.broadcasted_iota(jnp.int32, shape, dim)


def one_hot(hit):
    return hit.astype(F32).astype(BF16)


def two_parts(x):
    high = x.astype(BF16)
    return high, (x - high.astype(F32)).astype(BF16)


def fold8(x, op):
    parts = [x[8 * i : 8 * i + 8] for i in range(x.shape[0] // 8)]
    while len(parts) > 1:
        parts = [op(parts[i], parts[i + 1]) for i in range(0, len(parts), 2)]
    return parts[0]


def kernel(
    off_hbm,
    q_hbm,
    k_hbm,
    v_hbm,
    g_hbm,
    out_ref,
    off_ref,
    q_ref,
    k_ref,
    v_ref,
    g_ref,
    send_few,
    send_kv,
    send_qg,
    few,
    few1,
    kv,
    qg,
    peer,
    keys2,
    rows2,
    stats2,
    kv_k,
    kv_v,
    k_t,
    out_kv,
    out_q,
    out_l1,
    out_few,
    fin_kv,
    fin_q,
    fin_l1,
    fin_few,
    score,
    dprob,
    dsc,
    acc,
    base_kv,
    few_sem,
    kv_sem,
    qg_sem,
    l1_sem,
    l2_sem,
    pass_sem,
    dq_sem,
    home_sem,
    home1_sem,
    home2_sem,
    load_sem,
):
    major = lax.axis_index("ctxa")
    minor = lax.axis_index("ctxb")
    head = minor % GROUP
    mate = (major // 2) * 4 + minor // GROUP

    def member(dx, dy):
        x = (head % 4 + dx) % 4
        y = (head // 4 + dy) % 2
        return y * 4 + x

    def at_head(other):
        return (major, (minor // GROUP) * GROUP + other)

    def at_mate(other):
        return ((other // 4) * 2 + major % 2, (other % 4) * GROUP + head)

    layer = mate // 2

    def at_layer(other):
        return ((other // 2) * 2 + major % 2, (other % 2) * (2 * GROUP) + minor % (2 * GROUP))

    ahead = [member(r % 4, r // 4) for r in range(GROUP)]
    behind = [member(4 - r % 4, r // 4) for r in range(GROUP)]
    sibling = (major + 1 - 2 * (major % 2), minor)
    paired = minor // GROUP + 1 - 2 * ((minor // GROUP) % 2)

    def at_paired(other):
        return (major, paired * GROUP + other)

    def remote(src, dst, sems, device):
        return pltpu.make_async_remote_copy(
            src_ref=src,
            dst_ref=dst,
            send_sem=sems[0],
            recv_sem=sems[1],
            device_id=device,
            device_id_type=MESH,
        )

    def pair_of(sem, *index):
        return (sem.at[(0, *index)], sem.at[(1, *index)])

    barrier = pltpu.get_barrier_semaphore()

    def greet(device):
        pl.semaphore_signal(barrier, inc=1, device_id=device, device_id_type=MESH)

    for r in MATES_FAR_FIRST:
        greet(at_mate((mate + r) % MATES))
    for r in FAR_FIRST:
        greet(at_paired(behind[r]))
    for r in FAR_FIRST:
        greet(at_head(ahead[r]))
    greet(sibling)
    loads = []
    for i, (src, dst) in enumerate(
        ((k_hbm, k_ref), (v_hbm, v_ref), (q_hbm, q_ref), (g_hbm, g_ref), (off_hbm, off_ref))
    ):
        load = pltpu.make_async_copy(src, dst, load_sem.at[i])
        load.start()
        loads.append(load)

    row = iota((ROWS, ROWS), 0)
    col = iota((ROWS, ROWS), 1)
    split = one_hot(col == jnp.where(row < HALF, 2 * row, 2 * row - (ROWS - 1)))
    low = iota((ROWS, PAIR), 1) < HEAD_DIM

    for load in loads:
        load.wait()
    order = [[None, None] for _ in range(HEADS)]
    for which, (x_ref, y_ref, packed) in enumerate(
        ((k_ref, v_ref, send_kv), (q_ref, g_ref, send_qg))
    ):
        x_all = dot(split, x_ref[...])
        y_all = dot(split, y_ref[...])
        for t in range(HEADS // 2):
            x = x_all[:, t * PAIR : (t + 1) * PAIR]
            y = y_all[:, t * PAIR : (t + 1) * PAIR]
            for h, both in (
                (2 * t, jnp.where(low, x, pltpu.roll(y, HEAD_DIM, 1))),
                (2 * t + 1, jnp.where(low, pltpu.roll(x, HEAD_DIM, 1), y)),
            ):
                even = off_ref[1, h] == 0
                first = jnp.where(even, both[:HALF], both[HALF:]).astype(BF16)
                second = jnp.where(even, both[HALF:], both[:HALF]).astype(BF16)
                packed[h, 0] = first
                packed[h, 1] = second
                order[h][which] = [first, second]
    tile_row = iota((TILE, 2 * ROWS), 0)
    tile_col = iota((TILE, 2 * ROWS), 1)
    wanted = (tile_row >> 2) * ROWS + (tile_row & 3) * 16
    for h in range(HEADS):
        place = ((off_ref[1, h] + off_ref[2, h]) % 2) * HALF + (off_ref[2, h] >> 1)
        hit = one_hot((tile_col == wanted + place) & (tile_row < 8))
        send_few[h] = dot(hit, jnp.concatenate(order[h][0] + order[h][1], axis=0)).astype(BF16)

    pl.semaphore_wait(barrier, 2 * (GROUP - 1) + MATES - 1 + 1)

    in_few, in_few1, in_kv, in_l1, in_qg = {}, {}, {}, {}, [{}, {}]
    for r in FAR_FIRST:
        few_dst = few.at[pl.ds(r * TILE, TILE), :]
        in_few[r] = remote(send_few.at[ahead[r]], few_dst, pair_of(few_sem, 0, r), at_head(ahead[r]))
    for r in (*FAR_FIRST, 0):
        few_dst = few1.at[pl.ds(r * TILE, TILE), :]
        in_few1[r] = remote(
            send_few.at[ahead[r]], few_dst, pair_of(few_sem, 1, r), at_paired(ahead[r])
        )
    for r in FAR_FIRST:
        kv_dst = kv.at[:, pl.ds(r * HALF, HALF), :]
        in_kv[r] = remote(send_kv.at[ahead[r]], kv_dst, pair_of(kv_sem, r), at_head(ahead[r]))
        for half in range(2):
            qg_dst = qg.at[half, pl.ds(r * HALF, HALF), :]
            in_qg[half][r] = remote(
                send_qg.at[ahead[r], half], qg_dst, pair_of(qg_sem, half, r), at_head(ahead[r])
            )
    for r in (*FAR_FIRST, 0):
        l1_dst = peer.at[pl.ds(r * HALF, HALF), :]
        in_l1[r] = remote(
            send_kv.at[ahead[r], 0], l1_dst, pair_of(l1_sem, r), at_paired(ahead[r])
        )
    inward = (in_few, in_few1, in_kv, in_qg[1], in_l1, in_qg[0])
    for copies in inward:
        for copy in copies.values():
            copy.start()
    few[:TILE] = send_few[head]
    kv[:, :HALF] = send_kv[head]
    qg[:, :HALF] = send_qg[head]

    off1 = off_ref[1, head]
    off2 = off_ref[2, head]
    inside = (off1 + off2) % 2 == 0
    base = jnp.where(inside, 0, WIDE) + (off2 >> 1)
    at = iota((FEW, KEYS), 0)
    pick = iota((FEW, KEYS), 1) == base + (at >> 2) * HALF + (at & 3) * 16
    at = iota((KEYS, FEW), 1)
    pick_t = one_hot(iota((KEYS, FEW), 0) == base + (at >> 2) * HALF + (at & 3) * 16)
    pick_low = one_hot(pick)
    at = iota((2 * FEW, GROUP * TILE), 0)
    gather = one_hot(
        iota((2 * FEW, GROUP * TILE), 1)
        == ((at % FEW) >> 2) * TILE + (at & 3) + jnp.where(at < FEW, 0, 4)
    )
    for copy in (*in_few.values(), *in_few1.values()):
        copy.wait_recv()
    picked = dot(gather, few[...])
    picked1 = dot(gather, few1[...])
    own_kv2 = picked[:FEW]
    own_qg2 = picked[FEW:]
    mate1 = mate + 1 - 2 * (mate % 2)
    keys2[0, mate] = own_kv2.astype(BF16)
    rows2[0, mate] = own_qg2.astype(BF16)
    keys2[0, mate1] = picked1[:FEW].astype(BF16)
    rows2[0, mate1] = picked1[FEW:].astype(BF16)
    level2_refs = (keys2, rows2, stats2)

    layers = []
    for i in range(2):
        layers.append([])
        for r in LAYERS_FAR_FIRST:
            block = level2_refs[i].at[0, pl.ds(layer * 2, 2)]
            copy = remote(block, block, pair_of(l2_sem, i, r), at_layer((layer + r) % LAYERS))
            copy.start()
            layers[i].append(copy)

    def level2_pass(i):
        ref = level2_refs[i]
        copy = remote(ref.at[0], ref.at[1], pair_of(pass_sem, i), sibling)
        copy.start()
        return copy

    for copy in in_kv.values():
        copy.wait_recv()
    lane_low = iota((1, PAIR), 1) < HEAD_DIM
    zero = jnp.zeros((), BF16)
    kv_all = kv[...].reshape(KEYS, PAIR)
    kv_k[:KEYS] = jnp.where(lane_low, kv_all, zero)
    kv_v[:KEYS] = jnp.where(lane_low, zero, kv_all)
    k_t[:, :KEYS] = kv_all.T[:HEAD_DIM]

    def stats(c):
        half = c // 2
        first = (c % 2) * COLS
        for r in range(max(1, first // HALF), first // HALF + SLOTS):
            in_qg[half][r].wait_recv()
        across = qg[half, first : first + COLS, :].T
        steps = range(0, depth_of(c), DEEP)
        high8 = jnp.full((8, COLS), LOWEST, F32)
        for j in steps:
            s = dot(kv_k[j : j + DEEP], across) * TO_EXP2
            score[c, j : j + DEEP] = s
            high8 = jnp.maximum(high8, fold8(s, jnp.maximum))
        high = jnp.max(high8, axis=0, keepdims=True)
        sum8 = jnp.zeros((8, COLS), F32)
        dot8 = jnp.zeros((8, COLS), F32)
        for j in steps:
            e = jnp.exp2(score[c, j : j + DEEP] - high)
            score[c, j : j + DEEP] = e
            d = dot(kv_v[j : j + DEEP], across)
            dprob[c, j : j + DEEP] = d
            sum8 = sum8 + weight(c, j) * fold8(e, jnp.add)
            dot8 = dot8 + weight(c, j) * fold8(e * d, jnp.add)
        return (
            high,
            jnp.sum(sum8, axis=0, keepdims=True),
            jnp.sum(dot8, axis=0, keepdims=True),
        )

    def depth_of(c):
        return KEYS + WIDE if c < 2 else KEYS

    def weight(c, j):
        return 2.0 if c < 2 and j < WIDE else 1.0

    found = [None] * 4
    for c in (2, 3):
        found[c] = stats(c)
    for copy in in_l1.values():
        copy.wait_recv()
    peer_all = peer[...]
    kv_k[KEYS:] = jnp.where(lane_low, peer_all, zero)
    kv_v[KEYS:] = jnp.where(lane_low, zero, peer_all)
    k_t[:, KEYS:] = peer_all.T[:HEAD_DIM]
    for c in (0, 1):
        found[c] = stats(c)

    for copy in layers[0]:
        copy.wait_recv()
    passed_keys = level2_pass(0)
    passed_keys.wait_recv()

    few_low = iota((FEW, PAIR), 1) < HEAD_DIM
    both2 = jnp.concatenate(
        [jnp.where(few_low, own_qg2, 0.0), jnp.where(few_low, 0.0, own_qg2)], axis=0
    )
    kv2 = keys2[...].reshape(KEYS, PAIR)
    far = dot_nt(both2.astype(BF16), kv2)
    s2 = far[:FEW] * TO_EXP2
    d2 = far[FEW:]
    high2 = jnp.max(s2, axis=1, keepdims=True)
    e2 = jnp.exp2(s2 - high2)
    sum2 = jnp.sum(e2, axis=1, keepdims=True)
    dot2 = jnp.sum(e2 * d2, axis=1, keepdims=True)

    high, sums, products = [
        jnp.concatenate([found[c][i] for c in range(4)], axis=1) for i in range(3)
    ]
    high2_row = jnp.max(jnp.where(pick, high2, LOWEST), axis=0, keepdims=True)
    sum2_row = jnp.sum(jnp.where(pick, sum2, 0.0), axis=0, keepdims=True)
    dot2_row = jnp.sum(jnp.where(pick, dot2, 0.0), axis=0, keepdims=True)
    top = jnp.maximum(high, high2_row)
    factor = jnp.exp2(high - top)
    factor2 = jnp.exp2(high2_row - top)
    total = factor * sums + factor2 * sum2_row
    inverse = 1.0 / total
    delta = (factor * products + factor2 * dot2_row) * inverse
    factor = factor * inverse
    lse = top + jnp.log(total) * math.log2(math.e)
    lse2 = jnp.sum(jnp.where(pick, lse, 0.0), axis=1, keepdims=True)
    delta2 = jnp.sum(jnp.where(pick, delta, 0.0), axis=1, keepdims=True)

    lanes = iota((FEW, PAIR), 1) == (mate % 4) * FEW + iota((FEW, PAIR), 0)
    stats2[0, mate] = jnp.where(
        iota((8, PAIR), 0) == 0,
        jnp.sum(jnp.where(lanes, lse2, 0.0), axis=0, keepdims=True),
        jnp.sum(jnp.where(lanes, delta2, 0.0), axis=0, keepdims=True),
    )
    stat_block = stats2.at[0, mate]
    stat_copies = []
    for r in MATES_FAR_FIRST:
        copy = remote(stat_block, stat_block, pair_of(l2_sem, 2, r), at_mate((mate + r) % MATES))
        copy.start()
        stat_copies.append(copy)
    for copy in layers[1]:
        copy.wait_recv()
    passed_rows = level2_pass(1)
    ds2 = jnp.exp2(s2 - lse2) * (d2 - delta2)
    dq2_parts = two_parts(dot(ds2.astype(BF16), kv2).T[:HEAD_DIM])

    out_copies = []

    def grads(c, start):
        half = c // 2
        first = (c % 2) * COLS
        columns = slice(c * COLS, (c + 1) * COLS)
        mine = qg[half, first : first + COLS, :]
        scaled_q = jnp.where(lane_low, mine * jnp.asarray(SCALE, BF16), zero)
        only_g = jnp.where(lane_low, zero, mine)
        depth = depth_of(c)
        for j in range(0, depth, DEEP):
            p = score[c, j : j + DEEP] * (weight(c, j) * factor[:, columns])
            ds = (p * (dprob[c, j : j + DEEP] - delta[:, columns])).astype(BF16)
            dsc[j : j + DEEP] = ds
            added = dot(ds, scaled_q) + dot(p.astype(BF16), only_g)
            acc[j : j + DEEP] = added if start else acc[j : j + DEEP] + added
        dq_t = dot(k_t[:, :depth], dsc[:depth])
        for part in dq2_parts:
            dq_t = dq_t + dot(part, pick_low[:, columns])
        dq = (dq_t * SCALE).T
        sides = [
            jnp.concatenate([dq[i * HALF + b : i * HALF + b + QUARTER] for i in range(SLOTS)], 0)
            for b in (0, QUARTER)
        ]
        rows = slice((c % 2) * SLOTS * QUARTER, (c % 2 + 1) * SLOTS * QUARTER)
        out_q[half, rows] = jnp.concatenate(sides, axis=1).astype(BF16)
        for r in range(first // HALF, first // HALF + SLOTS):
            if r == 0:
                fin_q[half, head] = out_q[half, :QUARTER]
            else:
                copy = remote(
                    out_q.at[half, pl.ds(r * QUARTER, QUARTER), :],
                    fin_q.at[half, head],
                    pair_of(dq_sem, half, r),
                    at_head(behind[r]),
                )
                copy.start()
                out_copies.append(copy)

    grads(0, True)
    grads(1, False)
    out_l1[...] = acc[KEYS:].astype(BF16)
    for r in (*FAR_FIRST, 0):
        copy = remote(
            out_l1.at[pl.ds(r * HALF, HALF), :],
            fin_l1.at[head],
            pair_of(home1_sem, r),
            at_paired(behind[r]),
        )
        copy.start()
        out_copies.append(copy)
    grads(2, False)
    grads(3, False)
    out_kv[...] = acc[:KEYS].astype(BF16).reshape(2, WIDE, PAIR)
    fin_kv[head] = out_kv[:, :HALF]
    for r in FAR_FIRST:
        copy = remote(
            out_kv.at[:, pl.ds(r * HALF, HALF), :],
            fin_kv.at[head],
            pair_of(home_sem, r),
            at_head(behind[r]),
        )
        copy.start()
        out_copies.append(copy)

    passed_rows.wait_recv()
    qg2 = rows2[...].reshape(KEYS, PAIR)
    back = dot_nt(
        jnp.concatenate(
            [jnp.where(few_low, own_kv2, 0.0), jnp.where(few_low, 0.0, own_kv2)], axis=0
        ).astype(BF16),
        qg2,
    )
    for copy in stat_copies:
        copy.wait_recv()
    passed_stats = level2_pass(2)
    passed_stats.wait_recv()
    tiles = []
    for c in range(2):
        for m in range(0, MATES, 4):
            tiles.append(
                (stats2[c, m] + stats2[c, m + 1]) + (stats2[c, m + 2] + stats2[c, m + 3])
            )
    tiles = jnp.concatenate(tiles, axis=1)
    p2 = jnp.exp2(back[:FEW] * TO_EXP2 - tiles[0:1])
    ds2 = p2 * (back[FEW:] - tiles[1:2])
    scaled_q2 = jnp.where(lane_low, qg2 * jnp.asarray(SCALE, BF16), zero)
    only_g2 = jnp.where(lane_low, zero, qg2)
    kv_grad2 = dot(ds2.astype(BF16), scaled_q2) + dot(p2.astype(BF16), only_g2)
    at = iota((GROUP * TILE, FEW), 0)
    deal = one_hot(
        (iota((GROUP * TILE, FEW), 1) == (at >> 4) * 4 + (at & (TILE - 1)))
        & ((at & (TILE - 1)) < 4)
    )
    out_few[...] = dot(deal, kv_grad2.astype(BF16)).astype(BF16)
    fin_few[head] = out_few[:TILE]
    few_copies = []
    for r in FAR_FIRST:
        copy = remote(
            out_few.at[pl.ds(r * TILE, TILE), :],
            fin_few.at[head],
            pair_of(home2_sem, r),
            at_head(behind[r]),
        )
        copy.start()
        few_copies.append(copy)

    for copies in inward:
        for copy in copies.values():
            copy.wait_send()
    for copy in (*layers[0], *layers[1], *stat_copies, passed_keys, passed_rows, passed_stats):
        copy.wait_send()

    for copy in out_copies:
        copy.wait()

    merge = one_hot(row == jnp.where(col < HALF, 2 * col, 2 * col - (ROWS - 1)))
    quarter_low = iota((QUARTER, PAIR), 1) < HEAD_DIM

    def ordered(h, first, second):
        even = off_ref[1, h] == 0
        return jnp.where(even, first, second), jnp.where(even, second, first)

    def ordered_q(h):
        return ordered(h, fin_q[0, h].astype(F32), fin_q[1, h].astype(F32))

    def ordered_kv(h):
        first = fin_kv[h, 0].astype(F32) + fin_l1[h].astype(F32)
        return jnp.concatenate(ordered(h, first, fin_kv[h, 1].astype(F32)), axis=0)

    for t in range(HEADS // 2):
        lanes = slice(t * PAIR, (t + 1) * PAIR)
        a = ordered_kv(2 * t)
        b = ordered_kv(2 * t + 1)
        dk = jnp.where(low, a, pltpu.roll(b, HEAD_DIM, 1))
        dv = jnp.where(low, pltpu.roll(a, HEAD_DIM, 1), b)
        for i, x in enumerate((dk, dv)):
            upper, lower = two_parts(x)
            base_kv[i, :, lanes] = dot(merge, upper) + dot(merge, lower)
        parts = []
        for a, b in zip(ordered_q(2 * t), ordered_q(2 * t + 1)):
            parts.append(jnp.where(quarter_low, a, pltpu.roll(b, HEAD_DIM, 1)))
            parts.append(jnp.where(quarter_low, pltpu.roll(a, HEAD_DIM, 1), b))
        dq = jnp.concatenate(parts, axis=0).astype(BF16)
        out_ref[0, :, lanes] = dot(merge, dq).astype(BF16)
    tile_low = iota((TILE, PAIR), 1) < HEAD_DIM
    hits = []
    for h in range(HEADS):
        tile_row = iota((ROWS, TILE), 0)
        tile_col = iota((ROWS, TILE), 1)
        hits.append(((tile_row == off_ref[2, h] + tile_col * FEW) & (tile_col < 4)).astype(F32))
    hits = [jnp.concatenate(hits[i : i + 2], axis=1).astype(BF16) for i in range(0, HEADS, 2)]

    for copy in few_copies:
        copy.wait()
    for t in range(HEADS // 2):
        lanes = slice(t * PAIR, (t + 1) * PAIR)
        a = fin_few[2 * t].astype(F32)
        b = fin_few[2 * t + 1].astype(F32)
        dk = (jnp.where(tile_low, a, 0.0), jnp.where(tile_low, 0.0, pltpu.roll(b, HEAD_DIM, 1)))
        dv = (jnp.where(tile_low, pltpu.roll(a, HEAD_DIM, 1), 0.0), jnp.where(tile_low, 0.0, b))
        for i, x in enumerate((dk, dv)):
            added = dot(hits[t], jnp.concatenate(x, axis=0).astype(BF16))
            out_ref[i + 1, :, lanes] = (base_kv[i, :, lanes] + added).astype(BF16)


def local(queries, keys, values, grad_out, offsets):
    width = HEADS * HEAD_DIM
    dma = pltpu.SemaphoreType.DMA

    def low_buffer(*shape):
        return pltpu.VMEM(shape, BF16)

    result = pl.pallas_call(
        kernel,
        out_shape=jax.ShapeDtypeStruct((3, ROWS, width), BF16),
        in_specs=[pl.BlockSpec(memory_space=pltpu.HBM)] * 5,
        out_specs=pl.BlockSpec(memory_space=pltpu.VMEM),
        scratch_shapes=[
            pltpu.SMEM((LEVELS, HEADS), jnp.int32),
            low_buffer(ROWS, width),
            low_buffer(ROWS, width),
            low_buffer(ROWS, width),
            low_buffer(ROWS, width),
            low_buffer(HEADS, TILE, PAIR),
            low_buffer(HEADS, 2, HALF, PAIR),
            low_buffer(HEADS, 2, HALF, PAIR),
            low_buffer(GROUP * TILE, PAIR),
            low_buffer(GROUP * TILE, PAIR),
            low_buffer(2, WIDE, PAIR),
            low_buffer(2, WIDE, PAIR),
            low_buffer(WIDE, PAIR),
            low_buffer(2, MATES, FEW, PAIR),
            low_buffer(2, MATES, FEW, PAIR),
            pltpu.VMEM((2, MATES, 8, PAIR), F32),
            low_buffer(KEYS + WIDE, PAIR),
            low_buffer(KEYS + WIDE, PAIR),
            low_buffer(HEAD_DIM, KEYS + WIDE),
            low_buffer(2, WIDE, PAIR),
            low_buffer(2, GROUP * QUARTER, PAIR),
            low_buffer(WIDE, PAIR),
            low_buffer(GROUP * TILE, PAIR),
            low_buffer(HEADS, 2, HALF, PAIR),
            low_buffer(2, HEADS, QUARTER, PAIR),
            low_buffer(HEADS, HALF, PAIR),
            low_buffer(HEADS, TILE, PAIR),
            pltpu.VMEM((4, KEYS + WIDE, COLS), F32),
            pltpu.VMEM((4, KEYS + WIDE, COLS), F32),
            low_buffer(KEYS + WIDE, COLS),
            pltpu.VMEM((KEYS + WIDE, PAIR), F32),
            pltpu.VMEM((2, ROWS, width), F32),
            dma((2, 2, GROUP)),
            dma((2, GROUP)),
            dma((2, 2, GROUP)),
            dma((2, GROUP)),
            dma((2, 3, MATES)),
            dma((2, 3)),
            dma((2, 2, GROUP)),
            dma((2, GROUP)),
            dma((2, GROUP)),
            dma((2, GROUP)),
            dma((5,)),
        ],
        compiler_params=pltpu.CompilerParams(
            collective_id=0, has_side_effects=True, vmem_limit_bytes=63 * 1024 * 1024
        ),
    )(offsets, queries, keys, values, grad_out)
    return result[0], result[1], result[2]


def solution(mesh):
    rows = P(("ctxa", "ctxb"), None)
    return jax.shard_map(
        local,
        mesh=mesh,
        in_specs=(rows, rows, rows, rows, P()),
        out_specs=(rows, rows, rows),
        check_vma=False,
    )
```

```python
import math

import jax
import jax.numpy as jnp
from jax import lax
from jax.experimental import pallas as pl
from jax.experimental.pallas import tpu as pltpu
from jax.sharding import PartitionSpec as P

HEADS = 8
HEAD_DIM = 64
KEYS = 1024
LEVELS = 3
ROWS = 128
HALF = ROWS // 2
GROUP = 8
MATES = 16
WIDE = 512
FEW = 32
TILE = 16
QUARTER = HALF // 2
PAIR = 2 * HEAD_DIM
SCALE = HEAD_DIM ** (-0.5)
TO_EXP2 = SCALE * math.log2(math.e)
LOWEST = -1e30
MESH = pl.DeviceIdType.MESH
F32 = jnp.float32
BF16 = jnp.bfloat16
COLS = 256
SLOTS = COLS // HALF
DEEP = 128
KINDS = 18
(
    FEW_OWN,
    FEW_PAIRED,
    KV,
    LEVEL1,
    QG,
    GATHER,
    PASS,
    STAT,
    HOME_DQ,
    HOME_KV,
    HOME1,
    HOME2,
) = (0, 1, 2, 3, 4, 8, 10, 13, 14, 15, 16, 17)
FAR_FIRST = (6, 2, 5, 7, 4, 1, 3)
LAYERS = 8
NEAR_LAYERS = (2, 6, 1, 7)
LAYERS_FAR_FIRST = (4, 3, 5, 2, 6, 1, 7)
MATES_FAR_FIRST = (9, 8, 7, 10, 6, 11, 5, 12, 4, 13, 3, 14, 2, 15, 1)


def dot(x, y):
    return jnp.dot(x, y, preferred_element_type=F32)


def dot_nt(x, y):
    return lax.dot_general(x, y, (((1,), (1,)), ((), ())), preferred_element_type=F32)


def iota(shape, dim):
    return lax.broadcasted_iota(jnp.int32, shape, dim)


def one_hot(hit):
    return hit.astype(F32).astype(BF16)


def two_parts(x):
    high = x.astype(BF16)
    return high, (x - high.astype(F32)).astype(BF16)


def fold8(x, op):
    parts = [x[8 * i : 8 * i + 8] for i in range(x.shape[0] // 8)]
    while len(parts) > 1:
        parts = [op(parts[i], parts[i + 1]) for i in range(0, len(parts), 2)]
    return parts[0]


def kernel(
    off_hbm,
    q_hbm,
    k_hbm,
    v_hbm,
    g_hbm,
    out_hbm,
    off_ref,
    in_ref,
    send_few,
    send_kv,
    send_qg,
    few,
    few1,
    kv,
    qg,
    peer,
    keys2,
    rows2,
    stats2,
    kv_k,
    kv_v,
    k_t,
    out_kv,
    out_q,
    out_l1,
    out_few,
    fin_kv,
    fin_q,
    fin_l1,
    fin_few,
    score,
    dprob,
    dsc,
    acc,
    base_kv,
    out_ref,
    send_sem,
    recv_sem,
    load_sem,
    hop_sem,
):
    loads = [
        pltpu.make_async_copy(src, in_ref.at[i], load_sem.at[0])
        for i, src in enumerate((k_hbm, v_hbm, q_hbm, g_hbm))
    ]
    loads.append(pltpu.make_async_copy(off_hbm, off_ref, load_sem.at[1]))
    for load in loads:
        load.start()

    major = lax.axis_index("ctxa")
    minor = lax.axis_index("ctxb")
    head = minor % GROUP
    mate = (major // 2) * 4 + minor // GROUP

    def member(dx, dy):
        x = (head % 4 + dx) % 4
        y = (head // 4 + dy) % 2
        return y * 4 + x

    def at_head(other):
        return (major, (minor // GROUP) * GROUP + other)

    def at_mate(other):
        return ((other // 4) * 2 + major % 2, (other % 4) * GROUP + head)

    layer = mate // 2

    def at_layer(other):
        return ((other // 2) * 2 + major % 2, (other % 2) * (2 * GROUP) + minor % (2 * GROUP))

    ahead = [member(r % 4, r // 4) for r in range(GROUP)]
    behind = [member(4 - r % 4, r // 4) for r in range(GROUP)]
    sibling = (major + 1 - 2 * (major % 2), minor)
    paired = minor // GROUP + 1 - 2 * ((minor // GROUP) % 2)

    def at_paired(other):
        return (major, paired * GROUP + other)

    def send(src, dst, kind, device):
        pltpu.make_async_remote_copy(
            src_ref=src,
            dst_ref=dst,
            send_sem=send_sem.at[kind],
            recv_sem=recv_sem.at[kind],
            device_id=device,
            device_id_type=MESH,
        ).start()

    def received(kind, amount):
        pltpu.make_async_copy(amount, amount, recv_sem.at[kind]).wait()

    def sent(kind, amount):
        pltpu.make_async_copy(amount, amount, send_sem.at[kind]).wait()

    barrier = pltpu.get_barrier_semaphore()

    def greet(device):
        pl.semaphore_signal(barrier, inc=1, device_id=device, device_id_type=MESH)

    for r in FAR_FIRST:
        greet(at_head(ahead[r]))
    for r in (*FAR_FIRST, 0):
        greet(at_paired(behind[r]))
    for r in NEAR_LAYERS:
        greet(at_layer((layer + r) % LAYERS))
    greet(sibling)
    row = iota((ROWS, ROWS), 0)
    col = iota((ROWS, ROWS), 1)
    split = one_hot(col == jnp.where(row < HALF, 2 * row, 2 * row - (ROWS - 1)))
    low = iota((ROWS, PAIR), 1) < HEAD_DIM

    pltpu.make_async_copy(in_ref, in_ref, load_sem.at[0]).wait()
    loads[4].wait()
    order = [[None, None] for _ in range(HEADS)]
    for which, packed in enumerate((send_kv, send_qg)):
        x_all = dot(split, in_ref[2 * which])
        y_all = dot(split, in_ref[2 * which + 1])
        for t in range(HEADS // 2):
            x = x_all[:, t * PAIR : (t + 1) * PAIR]
            y = y_all[:, t * PAIR : (t + 1) * PAIR]
            for h, both in (
                (2 * t, jnp.where(low, x, pltpu.roll(y, HEAD_DIM, 1))),
                (2 * t + 1, jnp.where(low, pltpu.roll(x, HEAD_DIM, 1), y)),
            ):
                even = off_ref[1, h] == 0
                first = jnp.where(even, both[:HALF], both[HALF:]).astype(BF16)
                second = jnp.where(even, both[HALF:], both[:HALF]).astype(BF16)
                packed[h, 0] = first
                packed[h, 1] = second
                order[h][which] = [first, second]
    tile_row = iota((TILE, 2 * ROWS), 0)
    tile_col = iota((TILE, 2 * ROWS), 1)
    wanted = (tile_row >> 2) * ROWS + (tile_row & 3) * 16
    for h in range(HEADS):
        place = ((off_ref[1, h] + off_ref[2, h]) % 2) * HALF + (off_ref[2, h] >> 1)
        hit = one_hot((tile_col == wanted + place) & (tile_row < 8))
        send_few[h] = dot(hit, jnp.concatenate(order[h][0] + order[h][1], axis=0)).astype(BF16)

    pl.semaphore_wait(barrier, GROUP - 1 + GROUP + len(NEAR_LAYERS) + 1)

    for r in FAR_FIRST:
        tile = few.at[pl.ds(r * TILE, TILE), :]
        send(send_few.at[ahead[r]], tile, FEW_OWN, at_head(ahead[r]))
    for r in (*FAR_FIRST, 0):
        tile = few1.at[pl.ds(r * TILE, TILE), :]
        send(send_few.at[ahead[r]], tile, FEW_PAIRED, at_paired(ahead[r]))
    for r in NEAR_LAYERS[:2]:
        pl.semaphore_signal(
            hop_sem, inc=1, device_id=at_layer((layer + r) % LAYERS), device_id_type=MESH
        )
    for r in FAR_FIRST:
        slot = kv.at[:, pl.ds(r * HALF, HALF), :]
        send(send_kv.at[ahead[r]], slot, KV, at_head(ahead[r]))
    for r in (*FAR_FIRST, 0):
        slot = peer.at[pl.ds(r * HALF, HALF), :]
        send(send_kv.at[ahead[r], 0], slot, LEVEL1, at_paired(ahead[r]))

    def block_kind(c):
        return QG + c

    for half in (1, 0):
        for r in FAR_FIRST:
            slot = qg.at[half, pl.ds(r * HALF, HALF), :]
            kind = block_kind(2 * half + r // SLOTS)
            send(send_qg.at[ahead[r], half], slot, kind, at_head(ahead[r]))
    few[:TILE] = send_few[head]
    kv[:, :HALF] = send_kv[head]
    qg[:, :HALF] = send_qg[head]

    off1 = off_ref[1, head]
    off2 = off_ref[2, head]
    inside = (off1 + off2) % 2 == 0
    base = jnp.where(inside, 0, WIDE) + (off2 >> 1)
    at = iota((FEW, KEYS), 0)
    pick = iota((FEW, KEYS), 1) == base + (at >> 2) * HALF + (at & 3) * 16
    at = iota((KEYS, FEW), 1)
    pick_t = one_hot(iota((KEYS, FEW), 0) == base + (at >> 2) * HALF + (at & 3) * 16)
    pick_low = one_hot(pick)
    at = iota((2 * FEW, GROUP * TILE), 0)
    gather = one_hot(
        iota((2 * FEW, GROUP * TILE), 1)
        == ((at % FEW) >> 2) * TILE + (at & 3) + jnp.where(at < FEW, 0, 4)
    )
    pl.semaphore_wait(hop_sem, 2)
    received(FEW_OWN, few.at[pl.ds(TILE, (GROUP - 1) * TILE)])
    received(FEW_PAIRED, few1)
    picked = dot(gather, few[...])
    picked1 = dot(gather, few1[...])
    own_kv2 = picked[:FEW]
    own_qg2 = picked[FEW:]
    mate1 = mate + 1 - 2 * (mate % 2)
    keys2[0, mate] = own_kv2.astype(BF16)
    rows2[0, mate] = own_qg2.astype(BF16)
    keys2[0, mate1] = picked1[:FEW].astype(BF16)
    rows2[0, mate1] = picked1[FEW:].astype(BF16)
    for i, ref in enumerate((keys2, rows2)):
        block = ref.at[0, pl.ds(layer * 2, 2)]
        for r in LAYERS_FAR_FIRST:
            send(block, block, GATHER + i, at_layer((layer + r) % LAYERS))
    other_layers = keys2.at[0, pl.ds(0, MATES - 2)]

    received(KV, kv.at[:, pl.ds(HALF, WIDE - HALF), :])
    lane_low = iota((1, PAIR), 1) < HEAD_DIM
    zero = jnp.zeros((), BF16)
    kv_all = kv[...].reshape(KEYS, PAIR)
    kv_k[:KEYS] = jnp.where(lane_low, kv_all, zero)
    kv_v[:KEYS] = jnp.where(lane_low, zero, kv_all)
    k_t[:, :KEYS] = kv_all.T[:HEAD_DIM]

    def block_slots(c):
        slots = SLOTS if c % 2 else SLOTS - 1
        return qg.at[c // 2, pl.ds(WIDE - COLS, slots * HALF), :]

    def stats(c):
        half = c // 2
        first = (c % 2) * COLS
        received(block_kind(c), block_slots(c))
        across = qg[half, first : first + COLS, :].T
        steps = range(0, depth_of(c), DEEP)
        high8 = jnp.full((8, COLS), LOWEST, F32)
        for j in steps:
            s = dot(kv_k[j : j + DEEP], across) * TO_EXP2
            score[c, j : j + DEEP] = s
            high8 = jnp.maximum(high8, fold8(s, jnp.maximum))
        high = jnp.max(high8, axis=0, keepdims=True)
        sum8 = jnp.zeros((8, COLS), F32)
        dot8 = jnp.zeros((8, COLS), F32)
        for j in steps:
            e = jnp.exp2(score[c, j : j + DEEP] - high)
            score[c, j : j + DEEP] = e
            d = dot(kv_v[j : j + DEEP], across)
            dprob[c, j : j + DEEP] = d
            sum8 = sum8 + weight(c, j) * fold8(e, jnp.add)
            dot8 = dot8 + weight(c, j) * fold8(e * d, jnp.add)
        return (
            high,
            jnp.sum(sum8, axis=0, keepdims=True),
            jnp.sum(dot8, axis=0, keepdims=True),
        )

    def depth_of(c):
        return KEYS + WIDE if c < 2 else KEYS

    def weight(c, j):
        return 2.0 if c < 2 and j < WIDE else 1.0

    received(LEVEL1, peer)
    peer_all = peer[...]
    kv_k[KEYS:] = jnp.where(lane_low, peer_all, zero)
    kv_v[KEYS:] = jnp.where(lane_low, zero, peer_all)
    k_t[:, KEYS:] = peer_all.T[:HEAD_DIM]
    found = [None] * 4
    for c in (2, 3):
        found[c] = stats(c)
    received(GATHER, other_layers)
    send(keys2.at[0], keys2.at[1], PASS, sibling)
    found[0] = stats(0)
    received(PASS, keys2.at[0])

    few_low = iota((FEW, PAIR), 1) < HEAD_DIM
    both2 = jnp.concatenate(
        [jnp.where(few_low, own_qg2, 0.0), jnp.where(few_low, 0.0, own_qg2)], axis=0
    ).astype(BF16)
    kv2 = keys2[...].reshape(KEYS, PAIR)
    here = dot_nt(both2, kv_all)
    near = dot_nt(both2, peer_all)
    far = dot_nt(both2, kv2)
    s_here = here[:FEW] * TO_EXP2
    s_near = jnp.where(inside, near[:FEW] * TO_EXP2, LOWEST)
    s2 = far[:FEW] * TO_EXP2
    d2 = far[FEW:]
    high2 = jnp.maximum(
        jnp.maximum(
            jnp.max(s_here, axis=1, keepdims=True), jnp.max(s_near, axis=1, keepdims=True)
        ),
        jnp.max(s2, axis=1, keepdims=True),
    )
    twice = jnp.where((iota((FEW, KEYS), 1) < WIDE) & inside, 2.0, 1.0)
    e_here = jnp.exp2(s_here - high2) * twice
    e_near = jnp.exp2(s_near - high2)
    e2 = jnp.exp2(s2 - high2)
    sum2 = jnp.sum(e2, axis=1, keepdims=True)
    dot2 = jnp.sum(e2 * d2, axis=1, keepdims=True)
    total2 = sum2 + jnp.sum(e_here, axis=1, keepdims=True) + jnp.sum(e_near, axis=1, keepdims=True)
    product2 = (
        dot2
        + jnp.sum(e_here * here[FEW:], axis=1, keepdims=True)
        + jnp.sum(e_near * near[FEW:], axis=1, keepdims=True)
    )
    lse2 = high2 + jnp.log(total2) * math.log2(math.e)
    delta2 = product2 / total2
    lanes = iota((FEW, PAIR), 1) == (mate % 4) * FEW + iota((FEW, PAIR), 0)
    stats2[0, mate] = jnp.where(
        iota((8, PAIR), 0) == 0,
        jnp.sum(jnp.where(lanes, lse2, 0.0), axis=0, keepdims=True),
        jnp.sum(jnp.where(lanes, delta2, 0.0), axis=0, keepdims=True),
    )
    stat_block = stats2.at[0, mate]
    for r in MATES_FAR_FIRST:
        send(stat_block, stat_block, STAT, at_mate((mate + r) % MATES))
    received(GATHER + 1, other_layers)
    send(rows2.at[0], rows2.at[1], PASS + 1, sibling)
    ds2 = jnp.exp2(s2 - lse2) * (d2 - delta2)
    dq2_parts = two_parts(dot(ds2.astype(BF16), kv2).T[:HEAD_DIM])

    found[1] = stats(1)

    high, sums, products = [
        jnp.concatenate([found[c][i] for c in range(4)], axis=1) for i in range(3)
    ]
    high2_row = jnp.max(jnp.where(pick, high2, LOWEST), axis=0, keepdims=True)
    sum2_row = jnp.sum(jnp.where(pick, sum2, 0.0), axis=0, keepdims=True)
    dot2_row = jnp.sum(jnp.where(pick, dot2, 0.0), axis=0, keepdims=True)
    top = jnp.maximum(high, high2_row)
    factor = jnp.exp2(high - top)
    factor2 = jnp.exp2(high2_row - top)
    inverse = 1.0 / (factor * sums + factor2 * sum2_row)
    delta = (factor * products + factor2 * dot2_row) * inverse
    factor = factor * inverse

    def grads(c, start):
        half = c // 2
        first = (c % 2) * COLS
        columns = slice(c * COLS, (c + 1) * COLS)
        mine = qg[half, first : first + COLS, :]
        scaled_q = jnp.where(lane_low, mine * jnp.asarray(SCALE, BF16), zero)
        only_g = jnp.where(lane_low, zero, mine)
        depth = depth_of(c)
        for j in range(0, depth, DEEP):
            p = score[c, j : j + DEEP] * (weight(c, j) * factor[:, columns])
            ds = (p * (dprob[c, j : j + DEEP] - delta[:, columns])).astype(BF16)
            dsc[j : j + DEEP] = ds
            added = dot(ds, scaled_q) + dot(p.astype(BF16), only_g)
            acc[j : j + DEEP] = added if start else acc[j : j + DEEP] + added
        dq_t = dot(k_t[:, :depth], dsc[:depth])
        for part in dq2_parts:
            dq_t = dq_t + dot(part, pick_low[:, columns])
        dq = (dq_t * SCALE).T
        sides = [
            jnp.concatenate([dq[i * HALF + b : i * HALF + b + QUARTER] for i in range(SLOTS)], 0)
            for b in (0, QUARTER)
        ]
        rows = slice((c % 2) * SLOTS * QUARTER, (c % 2 + 1) * SLOTS * QUARTER)
        out_q[half, rows] = jnp.concatenate(sides, axis=1).astype(BF16)
        for r in range(first // HALF, first // HALF + SLOTS):
            if r == 0:
                fin_q[half, head] = out_q[half, :QUARTER]
            else:
                slot = out_q.at[half, pl.ds(r * QUARTER, QUARTER), :]
                send(slot, fin_q.at[half, head], HOME_DQ, at_head(behind[r]))

    grads(0, True)
    grads(1, False)
    out_l1[...] = acc[KEYS:].astype(BF16)
    for r in (*FAR_FIRST, 0):
        slot = out_l1.at[pl.ds(r * HALF, HALF), :]
        send(slot, fin_l1.at[head], HOME1, at_paired(behind[r]))
    grads(2, False)
    grads(3, False)
    out_kv[...] = acc[:KEYS].astype(BF16).reshape(2, WIDE, PAIR)
    fin_kv[head] = out_kv[:, :HALF]
    for r in FAR_FIRST:
        slot = out_kv.at[:, pl.ds(r * HALF, HALF), :]
        send(slot, fin_kv.at[head], HOME_KV, at_head(behind[r]))

    received(PASS + 1, rows2.at[0])
    qg2 = rows2[...].reshape(KEYS, PAIR)
    back = dot_nt(
        jnp.concatenate(
            [jnp.where(few_low, own_kv2, 0.0), jnp.where(few_low, 0.0, own_kv2)], axis=0
        ).astype(BF16),
        qg2,
    )
    other_mates = stats2.at[0, pl.ds(0, MATES - 1)]
    received(STAT, other_mates)
    send(stats2.at[0], stats2.at[1], PASS + 2, sibling)
    received(PASS + 2, stats2.at[0])
    tiles = []
    for c in range(2):
        for m in range(0, MATES, 4):
            tiles.append(
                (stats2[c, m] + stats2[c, m + 1]) + (stats2[c, m + 2] + stats2[c, m + 3])
            )
    tiles = jnp.concatenate(tiles, axis=1)
    p2 = jnp.exp2(back[:FEW] * TO_EXP2 - tiles[0:1])
    ds2 = p2 * (back[FEW:] - tiles[1:2])
    scaled_q2 = jnp.where(lane_low, qg2 * jnp.asarray(SCALE, BF16), zero)
    only_g2 = jnp.where(lane_low, zero, qg2)
    kv_grad2 = dot(ds2.astype(BF16), scaled_q2) + dot(p2.astype(BF16), only_g2)
    at = iota((GROUP * TILE, FEW), 0)
    deal = one_hot(
        (iota((GROUP * TILE, FEW), 1) == (at >> 4) * 4 + (at & (TILE - 1)))
        & ((at & (TILE - 1)) < 4)
    )
    out_few[...] = dot(deal, kv_grad2.astype(BF16)).astype(BF16)
    fin_few[head] = out_few[:TILE]
    for r in FAR_FIRST:
        send(out_few.at[pl.ds(r * TILE, TILE), :], fin_few.at[head], HOME2, at_head(behind[r]))

    sent(FEW_OWN, few.at[pl.ds(TILE, (GROUP - 1) * TILE)])
    sent(FEW_PAIRED, few1)
    sent(KV, kv.at[:, pl.ds(HALF, WIDE - HALF), :])
    sent(LEVEL1, peer)
    for c in range(4):
        sent(block_kind(c), block_slots(c))
    sent(GATHER, other_layers)
    sent(GATHER + 1, other_layers)
    sent(PASS, keys2.at[0])
    sent(PASS + 1, rows2.at[0])
    sent(PASS + 2, stats2.at[0])
    sent(STAT, other_mates)

    others = pl.ds(0, HEADS - 1)
    for done in (received, sent):
        done(HOME_DQ, fin_q.at[:, others])
        done(HOME1, fin_l1)
        done(HOME_KV, fin_kv.at[others])

    merge = one_hot(row == jnp.where(col < HALF, 2 * col, 2 * col - (ROWS - 1)))
    quarter_low = iota((QUARTER, PAIR), 1) < HEAD_DIM

    def ordered(h, first, second):
        even = off_ref[1, h] == 0
        return jnp.where(even, first, second), jnp.where(even, second, first)

    def ordered_q(h):
        return ordered(h, fin_q[0, h].astype(F32), fin_q[1, h].astype(F32))

    def ordered_kv(h):
        first = fin_kv[h, 0].astype(F32) + fin_l1[h].astype(F32)
        return jnp.concatenate(ordered(h, first, fin_kv[h, 1].astype(F32)), axis=0)

    for t in range(HEADS // 2):
        lanes = slice(t * PAIR, (t + 1) * PAIR)
        a = ordered_kv(2 * t)
        b = ordered_kv(2 * t + 1)
        dk = jnp.where(low, a, pltpu.roll(b, HEAD_DIM, 1))
        dv = jnp.where(low, pltpu.roll(a, HEAD_DIM, 1), b)
        for i, x in enumerate((dk, dv)):
            upper, lower = two_parts(x)
            base_kv[i, :, lanes] = dot(merge, upper) + dot(merge, lower)
        parts = []
        for a, b in zip(ordered_q(2 * t), ordered_q(2 * t + 1)):
            parts.append(jnp.where(quarter_low, a, pltpu.roll(b, HEAD_DIM, 1)))
            parts.append(jnp.where(quarter_low, pltpu.roll(a, HEAD_DIM, 1), b))
        dq = jnp.concatenate(parts, axis=0).astype(BF16)
        out_ref[0, :, lanes] = dot(merge, dq).astype(BF16)
    stores = [pltpu.make_async_copy(out_ref.at[0], out_hbm.at[0], load_sem.at[2])]
    stores[0].start()
    tile_low = iota((TILE, PAIR), 1) < HEAD_DIM
    hits = []
    for h in range(HEADS):
        tile_row = iota((ROWS, TILE), 0)
        tile_col = iota((ROWS, TILE), 1)
        hits.append(((tile_row == off_ref[2, h] + tile_col * FEW) & (tile_col < 4)).astype(F32))
    hits = [jnp.concatenate(hits[i : i + 2], axis=1).astype(BF16) for i in range(0, HEADS, 2)]

    received(HOME2, fin_few.at[others])
    sent(HOME2, fin_few.at[others])
    for t in range(HEADS // 2):
        lanes = slice(t * PAIR, (t + 1) * PAIR)
        a = fin_few[2 * t].astype(F32)
        b = fin_few[2 * t + 1].astype(F32)
        dk = (jnp.where(tile_low, a, 0.0), jnp.where(tile_low, 0.0, pltpu.roll(b, HEAD_DIM, 1)))
        dv = (jnp.where(tile_low, pltpu.roll(a, HEAD_DIM, 1), 0.0), jnp.where(tile_low, 0.0, b))
        for i, x in enumerate((dk, dv)):
            added = dot(hits[t], jnp.concatenate(x, axis=0).astype(BF16))
            out_ref[i + 1, :, lanes] = (base_kv[i, :, lanes] + added).astype(BF16)
    stores.append(
        pltpu.make_async_copy(out_ref.at[pl.ds(1, 2)], out_hbm.at[pl.ds(1, 2)], load_sem.at[3])
    )
    stores[1].start()
    for store in stores:
        store.wait()


def local(queries, keys, values, grad_out, offsets):
    width = HEADS * HEAD_DIM
    dma = pltpu.SemaphoreType.DMA

    def low_buffer(*shape):
        return pltpu.VMEM(shape, BF16)

    result = pl.pallas_call(
        kernel,
        out_shape=jax.ShapeDtypeStruct((3, ROWS, width), BF16),
        in_specs=[pl.BlockSpec(memory_space=pltpu.HBM)] * 5,
        out_specs=pl.BlockSpec(memory_space=pltpu.HBM),
        scratch_shapes=[
            pltpu.SMEM((LEVELS, HEADS), jnp.int32),
            low_buffer(4, ROWS, width),
            low_buffer(HEADS, TILE, PAIR),
            low_buffer(HEADS, 2, HALF, PAIR),
            low_buffer(HEADS, 2, HALF, PAIR),
            low_buffer(GROUP * TILE, PAIR),
            low_buffer(GROUP * TILE, PAIR),
            low_buffer(2, WIDE, PAIR),
            low_buffer(2, WIDE, PAIR),
            low_buffer(WIDE, PAIR),
            low_buffer(2, MATES, FEW, PAIR),
            low_buffer(2, MATES, FEW, PAIR),
            pltpu.VMEM((2, MATES, 8, PAIR), F32),
            low_buffer(KEYS + WIDE, PAIR),
            low_buffer(KEYS + WIDE, PAIR),
            low_buffer(HEAD_DIM, KEYS + WIDE),
            low_buffer(2, WIDE, PAIR),
            low_buffer(2, GROUP * QUARTER, PAIR),
            low_buffer(WIDE, PAIR),
            low_buffer(GROUP * TILE, PAIR),
            low_buffer(HEADS, 2, HALF, PAIR),
            low_buffer(2, HEADS, QUARTER, PAIR),
            low_buffer(HEADS, HALF, PAIR),
            low_buffer(HEADS, TILE, PAIR),
            pltpu.VMEM((4, KEYS + WIDE, COLS), F32),
            pltpu.VMEM((4, KEYS + WIDE, COLS), F32),
            low_buffer(KEYS + WIDE, COLS),
            pltpu.VMEM((KEYS + WIDE, PAIR), F32),
            pltpu.VMEM((2, ROWS, width), F32),
            low_buffer(3, ROWS, width),
            dma((KINDS,)),
            dma((KINDS,)),
            dma((4,)),
            pltpu.SemaphoreType.REGULAR,
        ],
        compiler_params=pltpu.CompilerParams(
            collective_id=0, has_side_effects=True, vmem_limit_bytes=63 * 1024 * 1024
        ),
    )(offsets, queries, keys, values, grad_out)
    return result[0], result[1], result[2]


def solution(mesh):
    rows = P(("ctxa", "ctxb"), None)
    return jax.shard_map(
        local,
        mesh=mesh,
        in_specs=(rows, rows, rows, rows, P()),
        out_specs=(rows, rows, rows),
        check_vma=False,
    )
```

```python
import math

import jax
import jax.numpy as jnp
from jax import lax
from jax.experimental import pallas as pl
from jax.experimental.pallas import tpu as pltpu
from jax.sharding import PartitionSpec as P

HEADS = 8
HEAD_DIM = 64
KEYS = 1024
LEVELS = 3
ROWS = 128
HALF = ROWS // 2
GROUP = 8
MATES = 16
WIDE = 512
FEW = 32
TILE = 16
PAIR = 2 * HEAD_DIM
SCALE = HEAD_DIM ** (-0.5)
TO_EXP2 = SCALE * math.log2(math.e)
LOWEST = -1e30
MESH = pl.DeviceIdType.MESH
F32 = jnp.float32
BF16 = jnp.bfloat16
COLS = 256
SLOTS = COLS // HALF
DEEP = 128
HOME_ROWS = ROWS + HALF + HALF + TILE
KINDS = 18
(
    FEW_OWN,
    FEW_PAIRED,
    KV,
    LEVEL1,
    QG,
    GATHER,
    PASS,
    STAT,
    HOME_DQ,
    HOME_KV,
    HOME1,
    HOME2,
) = (0, 1, 2, 3, 4, 8, 10, 12, 13, 15, 16, 17)
FAR_FIRST = (6, 2, 5, 7, 4, 1, 3)
LAYERS = 8
NEAR_LAYERS = (2, 6, 1, 7)
LAYERS_FAR_FIRST = (4, 3, 5, 2, 6, 1, 7)
MATES_FAR_FIRST = (9, 8, 7, 10, 6, 11, 5, 12, 4, 13, 3, 14, 2, 15, 1)


def dot(x, y):
    return jnp.dot(x, y, preferred_element_type=F32)


def dot_nt(x, y):
    return lax.dot_general(x, y, (((1,), (1,)), ((), ())), preferred_element_type=F32)


def iota(shape, dim):
    return lax.broadcasted_iota(jnp.int32, shape, dim)


def one_hot(hit):
    return hit.astype(F32).astype(BF16)


def two_parts(x):
    high = x.astype(BF16)
    return high, (x - high.astype(F32)).astype(BF16)


def fold8(x, op):
    parts = [x[8 * i : 8 * i + 8] for i in range(x.shape[0] // 8)]
    while len(parts) > 1:
        parts = [op(parts[i], parts[i + 1]) for i in range(0, len(parts), 2)]
    return parts[0]


def kernel(
    off_hbm,
    q_hbm,
    k_hbm,
    v_hbm,
    g_hbm,
    fin,
    off_ref,
    in_ref,
    send_few,
    send_kv,
    send_qg,
    few,
    few1,
    kv,
    qg,
    peer,
    keys2,
    rows2,
    stats2,
    k_t,
    out_kv,
    out_q,
    out_l1,
    out_few,
    score,
    dprob,
    dsc,
    dq_t,
    acc,
    send_sem,
    recv_sem,
    load_sem,
    own_sem,
    hop_sem,
):
    loads = [
        pltpu.make_async_copy(src, in_ref.at[i], load_sem.at[0])
        for i, src in enumerate((k_hbm, v_hbm, q_hbm, g_hbm))
    ]
    loads.append(pltpu.make_async_copy(off_hbm, off_ref, load_sem.at[1]))
    for load in loads:
        load.start()

    major = lax.axis_index("ctxa")
    minor = lax.axis_index("ctxb")
    head = minor % GROUP
    mate = (major // 2) * 4 + minor // GROUP

    def member(dx, dy):
        x = (head % 4 + dx) % 4
        y = (head // 4 + dy) % 2
        return y * 4 + x

    def at_head(other):
        return (major, (minor // GROUP) * GROUP + other)

    def at_mate(other, flip=0):
        return ((other // 4) * 2 + (major + flip) % 2, (other % 4) * GROUP + head)

    layer = mate // 2

    def at_layer(other):
        return ((other // 2) * 2 + major % 2, (other % 2) * (2 * GROUP) + minor % (2 * GROUP))

    ahead = [member(r % 4, r // 4) for r in range(GROUP)]
    behind = [member(4 - r % 4, r // 4) for r in range(GROUP)]
    sibling = (major + 1 - 2 * (major % 2), minor)
    paired = minor // GROUP + 1 - 2 * ((minor // GROUP) % 2)

    def at_paired(other):
        return (major, paired * GROUP + other)

    def send(src, dst, kind, device):
        pltpu.make_async_remote_copy(
            src_ref=src,
            dst_ref=dst,
            send_sem=send_sem.at[kind],
            recv_sem=recv_sem.at[kind],
            device_id=device,
            device_id_type=MESH,
        ).start()

    def received(kind, amount):
        pltpu.make_async_copy(amount, amount, recv_sem.at[kind]).wait()

    def sent(kind, amount):
        pltpu.make_async_copy(amount, amount, send_sem.at[kind]).wait()

    barrier = pltpu.get_barrier_semaphore()

    def greet(device):
        pl.semaphore_signal(barrier, inc=1, device_id=device, device_id_type=MESH)

    for r in FAR_FIRST:
        greet(at_head(ahead[r]))
    for r in (*FAR_FIRST, 0):
        greet(at_paired(behind[r]))
    for r in NEAR_LAYERS:
        greet(at_layer((layer + r) % LAYERS))
    greet(sibling)
    row = iota((ROWS, ROWS), 0)
    col = iota((ROWS, ROWS), 1)
    split = one_hot(col == jnp.where(row < HALF, 2 * row, 2 * row - (ROWS - 1)))
    low = iota((ROWS, PAIR), 1) < HEAD_DIM

    pltpu.make_async_copy(in_ref, in_ref, load_sem.at[0]).wait()
    loads[4].wait()
    order = [[None, None] for _ in range(HEADS)]
    for which, packed in enumerate((send_kv, send_qg)):
        x_all = dot(split, in_ref[2 * which])
        y_all = dot(split, in_ref[2 * which + 1])
        for t in range(HEADS // 2):
            x = x_all[:, t * PAIR : (t + 1) * PAIR]
            y = y_all[:, t * PAIR : (t + 1) * PAIR]
            for h, both in (
                (2 * t, jnp.where(low, x, pltpu.roll(y, HEAD_DIM, 1))),
                (2 * t + 1, jnp.where(low, pltpu.roll(x, HEAD_DIM, 1), y)),
            ):
                even = off_ref[1, h] == 0
                first = jnp.where(even, both[:HALF], both[HALF:]).astype(BF16)
                second = jnp.where(even, both[HALF:], both[:HALF]).astype(BF16)
                packed[h, 0] = first
                packed[h, 1] = second
                order[h][which] = [first, second]
    tile_row = iota((TILE, 2 * ROWS), 0)
    tile_col = iota((TILE, 2 * ROWS), 1)
    wanted = (tile_row >> 2) * ROWS + (tile_row & 3) * 16
    for h in range(HEADS):
        place = ((off_ref[1, h] + off_ref[2, h]) % 2) * HALF + (off_ref[2, h] >> 1)
        hit = one_hot((tile_col == wanted + place) & (tile_row < 8))
        send_few[h] = dot(hit, jnp.concatenate(order[h][0] + order[h][1], axis=0)).astype(BF16)

    pl.semaphore_wait(barrier, GROUP - 1 + GROUP + len(NEAR_LAYERS) + 1)

    for r in FAR_FIRST:
        tile = few.at[pl.ds(r * TILE, TILE), :]
        send(send_few.at[ahead[r]], tile, FEW_OWN, at_head(ahead[r]))
    for r in (*FAR_FIRST, 0):
        tile = few1.at[pl.ds(r * TILE, TILE), :]
        send(send_few.at[ahead[r]], tile, FEW_PAIRED, at_paired(ahead[r]))
    for r in NEAR_LAYERS[:2]:
        pl.semaphore_signal(
            hop_sem,
            inc=1,
            device_id=at_layer((layer + r) % LAYERS),
            device_id_type=MESH,
        )
    for r in FAR_FIRST:
        slot = kv.at[:, pl.ds(r * HALF, HALF), :]
        send(send_kv.at[ahead[r]], slot, KV, at_head(ahead[r]))
    for r in (*FAR_FIRST, 0):
        slot = peer.at[pl.ds(r * HALF, HALF), :]
        send(send_kv.at[ahead[r], 0], slot, LEVEL1, at_paired(ahead[r]))

    def block_kind(c):
        return QG + c

    for half in (0, 1):
        for r in FAR_FIRST:
            slot = qg.at[half, pl.ds(r * HALF, HALF), :]
            kind = block_kind(2 * half + r // SLOTS)
            send(send_qg.at[ahead[r], half], slot, kind, at_head(ahead[r]))
    few[:TILE] = send_few[head]
    kv[:, :HALF] = send_kv[head]
    qg[:, :HALF] = send_qg[head]

    off1 = off_ref[1, head]
    off2 = off_ref[2, head]
    inside = (off1 + off2) % 2 == 0
    base = jnp.where(inside, 0, WIDE) + (off2 >> 1)
    at = iota((FEW, KEYS), 0)
    pick = iota((FEW, KEYS), 1) == base + (at >> 2) * HALF + (at & 3) * 16
    at = iota((KEYS, FEW), 1)
    pick_t = one_hot(iota((KEYS, FEW), 0) == base + (at >> 2) * HALF + (at & 3) * 16)
    pick_low = one_hot(pick)
    at = iota((2 * FEW, GROUP * TILE), 0)
    gather = one_hot(
        iota((2 * FEW, GROUP * TILE), 1)
        == ((at % FEW) >> 2) * TILE + (at & 3) + jnp.where(at < FEW, 0, 4)
    )
    pl.semaphore_wait(hop_sem, 2)
    received(FEW_OWN, few.at[pl.ds(TILE, (GROUP - 1) * TILE)])
    received(FEW_PAIRED, few1)
    picked = dot(gather, few[...])
    picked1 = dot(gather, few1[...])
    own_kv2 = picked[:FEW]
    own_qg2 = picked[FEW:]
    mate1 = mate + 1 - 2 * (mate % 2)
    keys2[mate] = own_kv2.astype(BF16)
    rows2[mate] = own_qg2.astype(BF16)
    keys2[mate1] = picked1[:FEW].astype(BF16)
    rows2[mate1] = picked1[FEW:].astype(BF16)
    block = keys2.at[pl.ds(layer * 2, 2)]
    for r in LAYERS_FAR_FIRST:
        send(block, block, GATHER, at_layer((layer + r) % LAYERS))
    other_layers = keys2.at[pl.ds(0, MATES - 2)]
    this_core = pl.ds(0, MATES)
    that_core = pl.ds(MATES, MATES)

    received(KV, kv.at[:, pl.ds(HALF, WIDE - HALF), :])
    lane_low = iota((1, PAIR), 1) < HEAD_DIM
    zero = jnp.zeros((), BF16)
    kv_all = kv[...].reshape(KEYS, PAIR)

    def block_slots(c):
        slots = SLOTS if c % 2 else SLOTS - 1
        return qg.at[c // 2, pl.ds(WIDE - COLS, slots * HALF), :]

    def key_rows(j):
        if j < KEYS:
            return kv[j // WIDE, j % WIDE : j % WIDE + DEEP]
        return peer[j - KEYS : j - KEYS + DEEP]

    def stats(c):
        half = c // 2
        first = (c % 2) * COLS
        across = qg[half, first : first + COLS, :].T
        across_low = iota((PAIR, COLS), 0) < HEAD_DIM
        across_q = jnp.where(across_low, across, zero)
        across_g = jnp.where(across_low, zero, across)
        steps = range(0, depth_of(c), DEEP)
        high8 = jnp.full((8, COLS), LOWEST, F32)
        for j in steps:
            s = dot(key_rows(j), across_q) * TO_EXP2
            score[c, j : j + DEEP] = s
            high8 = jnp.maximum(high8, fold8(s, jnp.maximum))
        high = jnp.max(high8, axis=0, keepdims=True)
        sum8 = jnp.zeros((8, COLS), F32)
        dot8 = jnp.zeros((8, COLS), F32)
        for j in steps:
            e = jnp.exp2(score[c, j : j + DEEP] - high)
            score[c, j : j + DEEP] = e
            d = dot(key_rows(j), across_g)
            dprob[c, j : j + DEEP] = d
            sum8 = sum8 + weight(c, j) * fold8(e, jnp.add)
            dot8 = dot8 + weight(c, j) * fold8(e * d, jnp.add)
        return (
            high,
            jnp.sum(sum8, axis=0, keepdims=True),
            jnp.sum(dot8, axis=0, keepdims=True),
        )

    def depth_of(c):
        return KEYS + WIDE if c < 2 else KEYS

    def weight(c, j):
        return 2.0 if c < 2 and j < WIDE else 1.0

    received(LEVEL1, peer)
    peer_all = peer[...]
    received(GATHER, other_layers)
    send(keys2.at[this_core], keys2.at[that_core], PASS, sibling)
    few_low = iota((FEW, PAIR), 1) < HEAD_DIM
    both2 = jnp.concatenate(
        [jnp.where(few_low, own_qg2, 0.0), jnp.where(few_low, 0.0, own_qg2)], axis=0
    ).astype(BF16)
    here = dot_nt(both2, kv_all)
    near = dot_nt(both2, peer_all)
    s_here = here[:FEW] * TO_EXP2
    s_near = jnp.where(inside, near[:FEW] * TO_EXP2, LOWEST)
    twice = jnp.where((iota((FEW, KEYS), 1) < WIDE) & inside, 2.0, 1.0)
    high_own = jnp.maximum(
        jnp.max(s_here, axis=1, keepdims=True), jnp.max(s_near, axis=1, keepdims=True)
    )
    e_here = jnp.exp2(s_here - high_own) * twice
    e_near = jnp.exp2(s_near - high_own)
    sum_own = jnp.sum(e_here, axis=1, keepdims=True) + jnp.sum(e_near, axis=1, keepdims=True)
    dot_own = jnp.sum(e_here * here[FEW:], axis=1, keepdims=True) + jnp.sum(
        e_near * near[FEW:], axis=1, keepdims=True
    )
    block = rows2.at[pl.ds(layer * 2, 2)]
    for r in LAYERS_FAR_FIRST:
        send(block, block, GATHER + 1, at_layer((layer + r) % LAYERS))
    for c in (0, 1):
        received(block_kind(c), block_slots(c))
    found = [stats(0), stats(1)]
    received(PASS, keys2.at[this_core])

    kv2 = keys2[...].reshape(KEYS, PAIR)
    far = dot_nt(both2, kv2)
    s2 = far[:FEW] * TO_EXP2
    d2 = far[FEW:]
    high2 = jnp.maximum(high_own, jnp.max(s2, axis=1, keepdims=True))
    e2 = jnp.exp2(s2 - high2)
    sum2 = jnp.sum(e2, axis=1, keepdims=True)
    dot2 = jnp.sum(e2 * d2, axis=1, keepdims=True)
    shift = jnp.exp2(high_own - high2)
    total2 = sum2 + shift * sum_own
    product2 = dot2 + shift * dot_own
    lse2 = high2 + jnp.log(total2) * math.log2(math.e)
    delta2 = product2 / total2
    lanes = iota((FEW, PAIR), 1) == (mate % 4) * FEW + iota((FEW, PAIR), 0)
    stats2[mate] = jnp.concatenate(
        [
            jnp.sum(jnp.where(lanes, lse2, 0.0), axis=0, keepdims=True),
            jnp.sum(jnp.where(lanes, delta2, 0.0), axis=0, keepdims=True),
        ],
        axis=0,
    )
    stat_block = stats2.at[mate]
    stat_block1 = stats2.at[MATES + mate]
    for r in MATES_FAR_FIRST:
        send(stat_block, stat_block, STAT, at_mate((mate + r) % MATES))
        send(stat_block, stat_block1, STAT, at_mate((mate + r) % MATES, 1))
    send(stat_block, stat_block1, STAT, sibling)
    other_stats = stats2.at[pl.ds(0, 2 * MATES - 1)]
    ds2 = jnp.exp2(s2 - lse2) * (d2 - delta2)
    dq2_parts = two_parts(dot(ds2.astype(BF16), kv2).T[:HEAD_DIM])

    high2_row = jnp.max(jnp.where(pick, high2, LOWEST), axis=0, keepdims=True)
    sum2_row = jnp.sum(jnp.where(pick, sum2, 0.0), axis=0, keepdims=True)
    dot2_row = jnp.sum(jnp.where(pick, dot2, 0.0), axis=0, keepdims=True)

    def grads(c, own):
        columns = slice(c * COLS, (c + 1) * COLS)
        high, total, product = own
        top = jnp.maximum(high, high2_row[:, columns])
        factor = jnp.exp2(high - top)
        factor2 = jnp.exp2(high2_row[:, columns] - top)
        inverse = 1.0 / (factor * total + factor2 * sum2_row[:, columns])
        delta = (factor * product + factor2 * dot2_row[:, columns]) * inverse
        factor = factor * inverse
        mine = qg[c // 2, (c % 2) * COLS : (c % 2 + 1) * COLS, :]
        scaled_q = jnp.where(lane_low, mine * jnp.asarray(SCALE, BF16), zero)
        only_g = jnp.where(lane_low, zero, mine)
        depth = depth_of(c)
        for j in range(0, depth, DEEP):
            p = score[c, j : j + DEEP] * (weight(c, j) * factor)
            ds = (p * (dprob[c, j : j + DEEP] - delta)).astype(BF16)
            dsc[c, j : j + DEEP] = ds
            added = dot(ds, scaled_q) + dot(p.astype(BF16), only_g)
            acc[j : j + DEEP] = added if c == 0 else acc[j : j + DEEP] + added
        dq_t[c // 2, :, (c % 2) * COLS : (c % 2 + 1) * COLS] = dot(k_t[:, :depth], dsc[c, :depth])

    def dq_home(half):
        columns = slice(half * WIDE, (half + 1) * WIDE)
        dq = dq_t[half] + dot(dq2_parts[0], pick_low[:, columns])
        dq = (dq + dot(dq2_parts[1], pick_low[:, columns])) * SCALE
        for i in range(0, WIDE, PAIR):
            two = jnp.concatenate([dq[:, i : i + PAIR], dq[:, i : i + PAIR]], axis=0).T
            for b in range(2):
                rows = two[b * HALF : (b + 1) * HALF]
                lanes_low = iota((HALF // 2, PAIR), 1) < HEAD_DIM
                out_q[half, i // HALF + b] = jnp.where(
                    lanes_low, rows[: HALF // 2], rows[HALF // 2 :]
                ).astype(BF16)
        place = pl.ds(ROWS + HALF + half * (HALF // 2), HALF // 2)
        for r in FAR_FIRST:
            send(out_q.at[half, r], fin.at[head, place], HOME_DQ + half, at_head(behind[r]))
        own = pltpu.make_async_copy(out_q.at[half, 0], fin.at[head, place], own_sem.at[half])
        own.start()
        return own

    k_t[:, :KEYS] = kv_all.T[:HEAD_DIM]
    k_t[:, KEYS:] = peer_all.T[:HEAD_DIM]
    grads(0, found[0])
    grads(1, found[1])
    out_l1[...] = acc[KEYS:].astype(BF16)
    for r in (*FAR_FIRST, 0):
        slot = out_l1.at[pl.ds(r * HALF, HALF), :]
        send(slot, fin.at[head, pl.ds(ROWS, HALF)], HOME1, at_paired(behind[r]))
    own_copies = [dq_home(0)]
    for c in (2, 3):
        received(block_kind(c), block_slots(c))
    found = [stats(2), stats(3)]
    grads(2, found[0])
    grads(3, found[1])
    for r in range(GROUP):
        for half in range(2):
            rows = slice(half * WIDE + r * HALF, half * WIDE + (r + 1) * HALF)
            out_kv[r, half * HALF : (half + 1) * HALF] = acc[rows].astype(BF16)
    for r in FAR_FIRST:
        send(out_kv.at[r], fin.at[head, pl.ds(0, ROWS)], HOME_KV, at_head(behind[r]))
    own_copies.append(
        pltpu.make_async_copy(out_kv.at[0], fin.at[head, pl.ds(0, ROWS)], own_sem.at[2])
    )
    own_copies[-1].start()
    received(GATHER + 1, other_layers)
    send(rows2.at[this_core], rows2.at[that_core], PASS + 1, sibling)
    own_copies.append(dq_home(1))

    received(PASS + 1, rows2.at[this_core])
    qg2 = rows2[...].reshape(KEYS, PAIR)
    back = dot_nt(
        jnp.concatenate(
            [jnp.where(few_low, own_kv2, 0.0), jnp.where(few_low, 0.0, own_kv2)], axis=0
        ).astype(BF16),
        qg2,
    )
    scaled_q2 = jnp.where(lane_low, qg2 * jnp.asarray(SCALE, BF16), zero)
    only_g2 = jnp.where(lane_low, zero, qg2)
    at = iota((GROUP * TILE, FEW), 0)
    deal = one_hot(
        (iota((GROUP * TILE, FEW), 1) == (at >> 4) * 4 + (at & (TILE - 1)))
        & ((at & (TILE - 1)) < 4)
    )
    received(STAT, other_stats)
    tiles = []
    for m in range(0, 2 * MATES, 4):
        tiles.append((stats2[m] + stats2[m + 1]) + (stats2[m + 2] + stats2[m + 3]))
    tiles = jnp.concatenate(tiles, axis=1)
    p2 = jnp.exp2(back[:FEW] * TO_EXP2 - tiles[0:1])
    ds2 = p2 * (back[FEW:] - tiles[1:2])
    kv_grad2 = dot(ds2.astype(BF16), scaled_q2) + dot(p2.astype(BF16), only_g2)
    out_few[...] = dot(deal, kv_grad2.astype(BF16)).astype(BF16)
    place = pl.ds(HOME_ROWS - TILE, TILE)
    for r in FAR_FIRST:
        tile = out_few.at[pl.ds(r * TILE, TILE), :]
        send(tile, fin.at[head, place], HOME2, at_head(behind[r]))
    own_copies.append(
        pltpu.make_async_copy(out_few.at[pl.ds(0, TILE), :], fin.at[head, place], own_sem.at[3])
    )
    own_copies[-1].start()

    sent(FEW_OWN, few.at[pl.ds(TILE, (GROUP - 1) * TILE)])
    sent(FEW_PAIRED, few1)
    sent(KV, kv.at[:, pl.ds(HALF, WIDE - HALF), :])
    sent(LEVEL1, peer)
    for c in range(4):
        sent(block_kind(c), block_slots(c))
    sent(GATHER, other_layers)
    sent(GATHER + 1, other_layers)
    sent(PASS, keys2.at[this_core])
    sent(PASS + 1, rows2.at[this_core])
    sent(STAT, other_stats)

    for done in (received, sent):
        for half in range(2):
            done(HOME_DQ + half, out_q.at[half, pl.ds(1, GROUP - 1)])
        done(HOME1, out_l1)
        done(HOME_KV, out_kv.at[pl.ds(1, GROUP - 1)])
    for copy in own_copies:
        copy.wait()
    for done in (received, sent):
        done(HOME2, out_few.at[pl.ds(TILE, (GROUP - 1) * TILE), :])


def finish(off_hbm, fin_hbm, dq_hbm, dk_hbm, dv_hbm, off_ref, fin, held, load_sem, store_sem):
    loads = [
        pltpu.make_async_copy(fin_hbm.at[pl.ds(h, 2)], fin.at[pl.ds(h, 2)], load_sem.at[h // 2])
        for h in range(0, HEADS, 2)
    ]
    loads.append(pltpu.make_async_copy(off_hbm, off_ref, load_sem.at[HEADS // 2]))
    for load in loads:
        load.start()
    row = iota((ROWS, ROWS), 0)
    col = iota((ROWS, ROWS), 1)
    merge = one_hot(row == jnp.where(col < HALF, 2 * col, 2 * col - (ROWS - 1)))
    low = iota((ROWS, PAIR), 1) < HEAD_DIM
    half_low = iota((HALF, PAIR), 1) < HEAD_DIM
    tile_row = iota((ROWS, TILE), 0)
    tile_col = iota((ROWS, TILE), 1)
    loads[-1].wait()

    def ordered(h, first, second):
        even = off_ref[1, h] == 0
        return jnp.where(even, first, second), jnp.where(even, second, first)

    def ordered_kv(h):
        place = ((off_ref[1, h] + off_ref[2, h]) % 2) * HALF + (off_ref[2, h] >> 1)
        hit = one_hot((tile_row == place + tile_col * 16) & (tile_col < 4))
        level2 = dot(hit, fin[h, HOME_ROWS - TILE :])
        first = fin[h, :HALF].astype(F32) + fin[h, ROWS : ROWS + HALF].astype(F32) + level2[:HALF]
        second = fin[h, HALF:ROWS].astype(F32) + level2[HALF:]
        return jnp.concatenate(ordered(h, first, second), axis=0)

    def ordered_q(h, side):
        halves = []
        for half in range(2):
            start = ROWS + HALF + half * (HALF // 2)
            x = fin[h, start : start + HALF // 2].astype(F32)
            turned = pltpu.roll(x, HEAD_DIM, 1)
            halves.append(jnp.concatenate([turned, x] if side else [x, turned], axis=0))
        return ordered(h, *halves)

    for load in loads[:-1]:
        load.wait()
    stores = []

    def store(i, parts, result):
        for t, x in enumerate(parts):
            lanes = slice(t * PAIR, (t + 1) * PAIR)
            held[i, :, lanes] = dot(merge, x.astype(BF16)).astype(BF16)
        stores.append(pltpu.make_async_copy(held.at[i], result, store_sem.at[i]))
        stores[-1].start()

    parts = []
    for t in range(HEADS // 2):
        a = ordered_q(2 * t, 0)
        b = ordered_q(2 * t + 1, 1)
        both = [jnp.where(half_low, a[i], b[i]) for i in range(2)]
        parts.append(jnp.concatenate(both, axis=0))
    store(0, parts, dq_hbm)
    heads = [ordered_kv(h) for h in range(HEADS)]
    pairs = [(heads[h], heads[h + 1]) for h in range(0, HEADS, 2)]
    store(1, [jnp.where(low, a, pltpu.roll(b, HEAD_DIM, 1)) for a, b in pairs], dk_hbm)
    store(2, [jnp.where(low, pltpu.roll(a, HEAD_DIM, 1), b) for a, b in pairs], dv_hbm)
    for copy in stores:
        copy.wait()


def local(queries, keys, values, grad_out, offsets):
    width = HEADS * HEAD_DIM
    dma = pltpu.SemaphoreType.DMA

    def low_buffer(*shape):
        return pltpu.VMEM(shape, BF16)

    result = pl.pallas_call(
        kernel,
        out_shape=jax.ShapeDtypeStruct((HEADS, HOME_ROWS, PAIR), BF16),
        in_specs=[pl.BlockSpec(memory_space=pltpu.HBM)] * 5,
        out_specs=pl.BlockSpec(memory_space=pltpu.HBM),
        scratch_shapes=[
            pltpu.SMEM((LEVELS, HEADS), jnp.int32),
            low_buffer(4, ROWS, width),
            low_buffer(HEADS, TILE, PAIR),
            low_buffer(HEADS, 2, HALF, PAIR),
            low_buffer(HEADS, 2, HALF, PAIR),
            low_buffer(GROUP * TILE, PAIR),
            low_buffer(GROUP * TILE, PAIR),
            low_buffer(2, WIDE, PAIR),
            low_buffer(2, WIDE, PAIR),
            low_buffer(WIDE, PAIR),
            low_buffer(2 * MATES, FEW, PAIR),
            low_buffer(2 * MATES, FEW, PAIR),
            pltpu.VMEM((2 * MATES, 2, PAIR), F32),
            low_buffer(HEAD_DIM, KEYS + WIDE),
            low_buffer(GROUP, ROWS, PAIR),
            low_buffer(2, GROUP, HALF // 2, PAIR),
            low_buffer(WIDE, PAIR),
            low_buffer(GROUP * TILE, PAIR),
            pltpu.VMEM((4, KEYS + WIDE, COLS), F32),
            pltpu.VMEM((4, KEYS + WIDE, COLS), F32),
            low_buffer(4, KEYS + WIDE, COLS),
            pltpu.VMEM((2, HEAD_DIM, WIDE), F32),
            pltpu.VMEM((KEYS + WIDE, PAIR), F32),
            dma((KINDS,)),
            dma((KINDS,)),
            dma((2,)),
            dma((4,)),
            pltpu.SemaphoreType.REGULAR,
        ],
        compiler_params=pltpu.CompilerParams(
            collective_id=0, has_side_effects=True, vmem_limit_bytes=63 * 1024 * 1024
        ),
    )(offsets, queries, keys, values, grad_out)
    one = jax.ShapeDtypeStruct((ROWS, width), BF16)
    hbm = pl.BlockSpec(memory_space=pltpu.HBM)
    return pl.pallas_call(
        finish,
        out_shape=(one, one, one),
        in_specs=[hbm, hbm],
        out_specs=(hbm, hbm, hbm),
        scratch_shapes=[
            pltpu.SMEM((LEVELS, HEADS), jnp.int32),
            low_buffer(HEADS, HOME_ROWS, PAIR),
            low_buffer(3, ROWS, width),
            dma((HEADS // 2 + 1,)),
            dma((3,)),
        ],
        compiler_params=pltpu.CompilerParams(vmem_limit_bytes=63 * 1024 * 1024),
    )(offsets, result)


def solution(mesh):
    rows = P(("ctxa", "ctxb"), None)
    return jax.shard_map(
        local,
        mesh=mesh,
        in_specs=(rows, rows, rows, rows, P()),
        out_specs=(rows, rows, rows),
        check_vma=False,
    )
```

```python
import math

import jax
import jax.numpy as jnp
from jax import lax
from jax.experimental import pallas as pl
from jax.experimental.pallas import tpu as pltpu
from jax.sharding import PartitionSpec as P

HEADS = 8
HEAD_DIM = 64
KEYS = 1024
LEVELS = 3
ROWS = 128
HALF = ROWS // 2
GROUP = 8
MATES = 16
WIDE = 512
FEW = 32
TILE = 16
PAIR = 2 * HEAD_DIM
SCALE = HEAD_DIM ** (-0.5)
TO_EXP2 = SCALE * math.log2(math.e)
LOWEST = -1e30
MESH = pl.DeviceIdType.MESH
F32 = jnp.float32
BF16 = jnp.bfloat16
COLS = 256
SLOTS = COLS // HALF
DEEP = 128
QUARTER = HALF // 2
HOME_L1_ROW = ROWS
HOME_DQ_ROW = HOME_L1_ROW + HALF
HOME_L2_ROW = HOME_DQ_ROW + HALF
HOME_ROWS = HOME_L2_ROW + TILE
KINDS = 24
(
    FEW_OWN,
    FEW_PAIRED,
    KV,
    LEVEL1,
    QG,
    GATHER,
    ROWS2,
    PASS,
    STAT,
    HOME_DQ,
    HOME_KV,
    HOME1,
    HOME2,
) = (0, 1, 2, 3, 4, 8, 16, 17, 19, 20, 21, 22, 23)
FAR_FIRST = (6, 2, 5, 7, 4, 1, 3)
LAYERS = 8
NEAR_LAYERS = (2, 6, 1, 7)
LAYERS_FAR_FIRST = (4, 3, 5, 2, 6, 1, 7)
MATES_FAR_FIRST = (9, 8, 7, 10, 6, 11, 5, 12, 4, 13, 3, 14, 2, 15, 1)


def dot(x, y):
    return jnp.dot(x, y, preferred_element_type=F32)


def dot_nt(x, y):
    return lax.dot_general(x, y, (((1,), (1,)), ((), ())), preferred_element_type=F32)


def iota(shape, dim):
    return lax.broadcasted_iota(jnp.int32, shape, dim)


def one_hot(hit):
    return hit.astype(F32).astype(BF16)


def two_parts(x):
    high = x.astype(BF16)
    return high, (x - high.astype(F32)).astype(BF16)


def fold8(x, op):
    parts = [x[8 * i : 8 * i + 8] for i in range(x.shape[0] // 8)]
    while len(parts) > 1:
        parts = [op(parts[i], parts[i + 1]) for i in range(0, len(parts), 2)]
    return parts[0]


def kernel(
    off_hbm,
    q_hbm,
    k_hbm,
    v_hbm,
    g_hbm,
    fin,
    off_ref,
    in_ref,
    send_few,
    send_kv,
    send_qg,
    few,
    few1,
    kv,
    qg,
    peer,
    keys2,
    rows2,
    stats2,
    k_t,
    out_kv,
    out_q,
    out_l1,
    out_few,
    score,
    dprob,
    dsc,
    dq_t,
    acc,
    send_sem,
    recv_sem,
    load_sem,
    own_sem,
    hop_sem,
):
    loads = [
        pltpu.make_async_copy(src, in_ref.at[i], load_sem.at[0])
        for i, src in enumerate((k_hbm, v_hbm, q_hbm, g_hbm))
    ]
    loads.append(pltpu.make_async_copy(off_hbm, off_ref, load_sem.at[1]))
    for load in loads:
        load.start()

    major = lax.axis_index("ctxa")
    minor = lax.axis_index("ctxb")
    head = minor % GROUP
    mate = (major // 2) * 4 + minor // GROUP

    def member(dx, dy):
        x = (head % 4 + dx) % 4
        y = (head // 4 + dy) % 2
        return y * 4 + x

    def at_head(other):
        return (major, (minor // GROUP) * GROUP + other)

    def at_mate(other, flip=0):
        return ((other // 4) * 2 + (major + flip) % 2, (other % 4) * GROUP + head)

    layer = mate // 2

    def at_layer(other):
        return ((other // 2) * 2 + major % 2, (other % 2) * (2 * GROUP) + minor % (2 * GROUP))

    ahead = [member(r % 4, r // 4) for r in range(GROUP)]
    behind = [member(4 - r % 4, r // 4) for r in range(GROUP)]
    sibling = (major + 1 - 2 * (major % 2), minor)
    paired = minor // GROUP + 1 - 2 * ((minor // GROUP) % 2)

    def at_paired(other):
        return (major, paired * GROUP + other)

    def send(src, dst, kind, device):
        pltpu.make_async_remote_copy(
            src_ref=src,
            dst_ref=dst,
            send_sem=send_sem.at[kind],
            recv_sem=recv_sem.at[kind],
            device_id=device,
            device_id_type=MESH,
        ).start()

    def received(kind, amount):
        pltpu.make_async_copy(amount, amount, recv_sem.at[kind]).wait()

    def sent(kind, amount):
        pltpu.make_async_copy(amount, amount, send_sem.at[kind]).wait()

    barrier = pltpu.get_barrier_semaphore()

    def greet(device):
        pl.semaphore_signal(barrier, inc=1, device_id=device, device_id_type=MESH)

    for r in FAR_FIRST:
        greet(at_head(ahead[r]))
    for r in (*FAR_FIRST, 0):
        greet(at_paired(behind[r]))
    for r in NEAR_LAYERS:
        greet(at_layer((layer + r) % LAYERS))
    greet(sibling)
    row = iota((ROWS, ROWS), 0)
    col = iota((ROWS, ROWS), 1)
    split = one_hot(col == jnp.where(row < HALF, 2 * row, 2 * row - (ROWS - 1)))
    low = iota((ROWS, PAIR), 1) < HEAD_DIM

    pltpu.make_async_copy(in_ref, in_ref, load_sem.at[0]).wait()
    loads[4].wait()
    order = [[None, None] for _ in range(HEADS)]
    for which, packed in enumerate((send_kv, send_qg)):
        x_all = dot(split, in_ref[2 * which])
        y_all = dot(split, in_ref[2 * which + 1])
        for t in range(HEADS // 2):
            x = x_all[:, t * PAIR : (t + 1) * PAIR]
            y = y_all[:, t * PAIR : (t + 1) * PAIR]
            for h, both in (
                (2 * t, jnp.where(low, x, pltpu.roll(y, HEAD_DIM, 1))),
                (2 * t + 1, jnp.where(low, pltpu.roll(x, HEAD_DIM, 1), y)),
            ):
                even = off_ref[1, h] == 0
                first = jnp.where(even, both[:HALF], both[HALF:]).astype(BF16)
                second = jnp.where(even, both[HALF:], both[:HALF]).astype(BF16)
                packed[h, 0] = first
                packed[h, 1] = second
                order[h][which] = [first, second]
    tile_row = iota((TILE, 2 * ROWS), 0)
    tile_col = iota((TILE, 2 * ROWS), 1)
    wanted = (tile_row >> 2) * ROWS + (tile_row & 3) * 16
    for h in range(HEADS):
        place = ((off_ref[1, h] + off_ref[2, h]) % 2) * HALF + (off_ref[2, h] >> 1)
        hit = one_hot((tile_col == wanted + place) & (tile_row < 8))
        send_few[h] = dot(hit, jnp.concatenate(order[h][0] + order[h][1], axis=0)).astype(BF16)

    pl.semaphore_wait(barrier, GROUP - 1 + GROUP + len(NEAR_LAYERS) + 1)

    for r in FAR_FIRST:
        tile = few.at[pl.ds(r * TILE, TILE), :]
        send(send_few.at[ahead[r]], tile, FEW_OWN, at_head(ahead[r]))
    for r in (*FAR_FIRST, 0):
        tile = few1.at[pl.ds(r * TILE, TILE), :]
        send(send_few.at[ahead[r]], tile, FEW_PAIRED, at_paired(ahead[r]))
    for r in NEAR_LAYERS[:2]:
        pl.semaphore_signal(
            hop_sem,
            inc=1,
            device_id=at_layer((layer + r) % LAYERS),
            device_id_type=MESH,
        )
    for r in FAR_FIRST:
        slot = kv.at[:, pl.ds(r * HALF, HALF), :]
        send(send_kv.at[ahead[r]], slot, KV, at_head(ahead[r]))
    for r in (*FAR_FIRST, 0):
        slot = peer.at[pl.ds(r * HALF, HALF), :]
        send(send_kv.at[ahead[r], 0], slot, LEVEL1, at_paired(ahead[r]))

    def block_kind(c):
        return QG + c

    for half in (0, 1):
        for r in FAR_FIRST:
            slot = qg.at[half, pl.ds(r * HALF, HALF), :]
            kind = block_kind(2 * half + r // SLOTS)
            send(send_qg.at[ahead[r], half], slot, kind, at_head(ahead[r]))
    few[:TILE] = send_few[head]
    kv[:, :HALF] = send_kv[head]
    qg[:, :HALF] = send_qg[head]

    off1 = off_ref[1, head]
    off2 = off_ref[2, head]
    inside = (off1 + off2) % 2 == 0
    base = jnp.where(inside, 0, WIDE) + (off2 >> 1)
    at = iota((FEW, KEYS), 0)
    pick = iota((FEW, KEYS), 1) == base + (at >> 2) * HALF + (at & 3) * 16
    at = iota((KEYS, FEW), 1)
    pick_t = one_hot(iota((KEYS, FEW), 0) == base + (at >> 2) * HALF + (at & 3) * 16)
    pick_low = one_hot(pick)
    at = iota((2 * FEW, GROUP * TILE), 0)
    gather = one_hot(
        iota((2 * FEW, GROUP * TILE), 1)
        == ((at % FEW) >> 2) * TILE + (at & 3) + jnp.where(at < FEW, 0, 4)
    )
    pl.semaphore_wait(hop_sem, 2)
    received(FEW_OWN, few.at[pl.ds(TILE, (GROUP - 1) * TILE)])
    received(FEW_PAIRED, few1)
    picked = dot(gather, few[...])
    picked1 = dot(gather, few1[...])
    own_kv2 = picked[:FEW]
    own_qg2 = picked[FEW:]
    mate1 = mate + 1 - 2 * (mate % 2)
    keys2[mate] = own_kv2.astype(BF16)
    rows2[mate] = own_qg2.astype(BF16)
    keys2[mate1] = picked1[:FEW].astype(BF16)
    rows2[mate1] = picked1[FEW:].astype(BF16)
    block = keys2.at[pl.ds(layer * 2, 2)]
    for r in LAYERS_FAR_FIRST:
        send(block, block, GATHER + layer, at_layer((layer + r) % LAYERS))
    send(block, keys2.at[pl.ds(MATES + layer * 2, 2)], PASS, sibling)
    other_layers = keys2.at[pl.ds(0, MATES - 2)]
    this_core = pl.ds(0, MATES)
    that_core = pl.ds(MATES, MATES)

    received(KV, kv.at[:, pl.ds(HALF, WIDE - HALF), :])
    lane_low = iota((1, PAIR), 1) < HEAD_DIM
    zero = jnp.zeros((), BF16)
    kv_all = kv[...].reshape(KEYS, PAIR)

    def block_slots(c):
        slots = SLOTS if c % 2 else SLOTS - 1
        return qg.at[c // 2, pl.ds(WIDE - COLS, slots * HALF), :]

    def key_rows(j):
        if j < KEYS:
            return kv[j // WIDE, j % WIDE : j % WIDE + DEEP]
        return peer[j - KEYS : j - KEYS + DEEP]

    def stats(c):
        half = c // 2
        first = (c % 2) * COLS
        across = qg[half, first : first + COLS, :].T
        across_low = iota((PAIR, COLS), 0) < HEAD_DIM
        across_q = jnp.where(across_low, across, zero)
        across_g = jnp.where(across_low, zero, across)
        steps = range(0, depth_of(c), DEEP)
        high8 = jnp.full((8, COLS), LOWEST, F32)
        for j in steps:
            s = dot(key_rows(j), across_q) * TO_EXP2
            score[c, j : j + DEEP] = s
            high8 = jnp.maximum(high8, fold8(s, jnp.maximum))
        high = jnp.max(high8, axis=0, keepdims=True)
        sum8 = jnp.zeros((8, COLS), F32)
        dot8 = jnp.zeros((8, COLS), F32)
        for j in steps:
            e = jnp.exp2(score[c, j : j + DEEP] - high)
            score[c, j : j + DEEP] = e
            d = dot(key_rows(j), across_g)
            dprob[c, j : j + DEEP] = d
            sum8 = sum8 + weight(c, j) * fold8(e, jnp.add)
            dot8 = dot8 + weight(c, j) * fold8(e * d, jnp.add)
        return (
            high,
            jnp.sum(sum8, axis=0, keepdims=True),
            jnp.sum(dot8, axis=0, keepdims=True),
        )

    def depth_of(c):
        return KEYS + WIDE if c < 2 else KEYS

    def weight(c, j):
        return 2.0 if c < 2 and j < WIDE else 1.0

    received(LEVEL1, peer)
    peer_all = peer[...]
    for i in range(LAYERS - 1):
        other = i + (i + LAYERS - layer) // LAYERS
        block = keys2.at[pl.ds(other * 2, 2)]
        received(GATHER + other, block)
        send(block, keys2.at[pl.ds(MATES + other * 2, 2)], PASS, sibling)
    few_low = iota((FEW, PAIR), 1) < HEAD_DIM
    both2 = jnp.concatenate(
        [jnp.where(few_low, own_qg2, 0.0), jnp.where(few_low, 0.0, own_qg2)], axis=0
    ).astype(BF16)
    here = dot_nt(both2, kv_all)
    near = dot_nt(both2, peer_all)
    s_here = here[:FEW] * TO_EXP2
    s_near = jnp.where(inside, near[:FEW] * TO_EXP2, LOWEST)
    twice = jnp.where((iota((FEW, KEYS), 1) < WIDE) & inside, 2.0, 1.0)
    high_own = jnp.maximum(
        jnp.max(s_here, axis=1, keepdims=True), jnp.max(s_near, axis=1, keepdims=True)
    )
    e_here = jnp.exp2(s_here - high_own) * twice
    e_near = jnp.exp2(s_near - high_own)
    sum_own = jnp.sum(e_here, axis=1, keepdims=True) + jnp.sum(e_near, axis=1, keepdims=True)
    dot_own = jnp.sum(e_here * here[FEW:], axis=1, keepdims=True) + jnp.sum(
        e_near * near[FEW:], axis=1, keepdims=True
    )
    block = rows2.at[pl.ds(layer * 2, 2)]
    for r in LAYERS_FAR_FIRST:
        send(block, block, ROWS2, at_layer((layer + r) % LAYERS))
    for c in (0, 1):
        received(block_kind(c), block_slots(c))
    found = [stats(0), stats(1)]
    k_t[:, :KEYS] = kv_all.T[:HEAD_DIM]
    k_t[:, KEYS:] = peer_all.T[:HEAD_DIM]
    received(PASS, keys2.at[this_core])

    kv2 = keys2[...].reshape(KEYS, PAIR)
    far = dot_nt(both2, kv2)
    s2 = far[:FEW] * TO_EXP2
    d2 = far[FEW:]
    high2 = jnp.maximum(high_own, jnp.max(s2, axis=1, keepdims=True))
    e2 = jnp.exp2(s2 - high2)
    sum2 = jnp.sum(e2, axis=1, keepdims=True)
    dot2 = jnp.sum(e2 * d2, axis=1, keepdims=True)
    shift = jnp.exp2(high_own - high2)
    total2 = sum2 + shift * sum_own
    product2 = dot2 + shift * dot_own
    lse2 = high2 + jnp.log(total2) * math.log2(math.e)
    delta2 = product2 / total2
    lanes = iota((FEW, PAIR), 1) == (mate % 4) * FEW + iota((FEW, PAIR), 0)
    stats2[mate] = jnp.concatenate(
        [
            jnp.sum(jnp.where(lanes, lse2, 0.0), axis=0, keepdims=True),
            jnp.sum(jnp.where(lanes, delta2, 0.0), axis=0, keepdims=True),
        ],
        axis=0,
    )
    stat_block = stats2.at[mate]
    stat_block1 = stats2.at[MATES + mate]
    for r in MATES_FAR_FIRST:
        send(stat_block, stat_block, STAT, at_mate((mate + r) % MATES))
        send(stat_block, stat_block1, STAT, at_mate((mate + r) % MATES, 1))
    send(stat_block, stat_block1, STAT, sibling)
    other_stats = stats2.at[pl.ds(0, 2 * MATES - 1)]
    high2_row = jnp.max(jnp.where(pick, high2, LOWEST), axis=0, keepdims=True)
    sum2_row = jnp.sum(jnp.where(pick, sum2, 0.0), axis=0, keepdims=True)
    dot2_row = jnp.sum(jnp.where(pick, dot2, 0.0), axis=0, keepdims=True)

    def grads(c, own):
        columns = slice(c * COLS, (c + 1) * COLS)
        high, total, product = own
        top = jnp.maximum(high, high2_row[:, columns])
        factor = jnp.exp2(high - top)
        factor2 = jnp.exp2(high2_row[:, columns] - top)
        inverse = 1.0 / (factor * total + factor2 * sum2_row[:, columns])
        delta = (factor * product + factor2 * dot2_row[:, columns]) * inverse
        factor = factor * inverse
        mine = qg[c // 2, (c % 2) * COLS : (c % 2 + 1) * COLS, :]
        scaled_q = jnp.where(lane_low, mine * jnp.asarray(SCALE, BF16), zero)
        only_g = jnp.where(lane_low, zero, mine)
        depth = depth_of(c)
        for j in range(0, depth, DEEP):
            p = score[c, j : j + DEEP] * (weight(c, j) * factor)
            ds = (p * (dprob[c, j : j + DEEP] - delta)).astype(BF16)
            dsc[c, j : j + DEEP] = ds
            added = dot(ds, scaled_q) + dot(p.astype(BF16), only_g)
            acc[j : j + DEEP] = added if c == 0 else acc[j : j + DEEP] + added
        dq_t[c // 2, :, (c % 2) * COLS : (c % 2 + 1) * COLS] = dot(k_t[:, :depth], dsc[c, :depth])

    def dq_pack(half):
        columns = slice(half * WIDE, (half + 1) * WIDE)
        dq = dq_t[half] + dot(dq2_parts[0], pick_low[:, columns])
        dq = (dq + dot(dq2_parts[1], pick_low[:, columns])) * SCALE
        lanes_low = iota((QUARTER, PAIR), 1) < HEAD_DIM
        for i in range(0, WIDE, PAIR):
            two = jnp.concatenate([dq[:, i : i + PAIR], dq[:, i : i + PAIR]], axis=0).T
            for b in range(2):
                rows = two[b * HALF : (b + 1) * HALF]
                packed = jnp.where(lanes_low, rows[:QUARTER], rows[QUARTER:]).astype(BF16)
                out_q[i // HALF + b, half * QUARTER : (half + 1) * QUARTER] = packed

    grads(0, found[0])
    grads(1, found[1])
    out_l1[...] = acc[KEYS:].astype(BF16)
    for r in (*FAR_FIRST, 0):
        slot = out_l1.at[pl.ds(r * HALF, HALF), :]
        send(slot, fin.at[head, pl.ds(HOME_L1_ROW, HALF)], HOME1, at_paired(behind[r]))

    def take_home(i, src, first, rows, kind):
        place = fin.at[head, pl.ds(first, rows)]
        for r in FAR_FIRST:
            send(src.at[r], place, kind, at_head(behind[r]))
        copy = pltpu.make_async_copy(src.at[0], place, own_sem.at[i])
        copy.start()
        return copy

    received(ROWS2, other_layers)
    send(rows2.at[this_core], rows2.at[that_core], PASS + 1, sibling)
    for c in (2, 3):
        received(block_kind(c), block_slots(c))
    found += [stats(2), stats(3)]
    grads(2, found[2])
    grads(3, found[3])
    for r in range(GROUP):
        for half in range(2):
            rows = slice(half * WIDE + r * HALF, half * WIDE + (r + 1) * HALF)
            out_kv[r, half * HALF : (half + 1) * HALF] = acc[rows].astype(BF16)
    own_copies = [take_home(0, out_kv, 0, ROWS, HOME_KV)]
    ds2 = jnp.exp2(s2 - lse2) * (d2 - delta2)
    dq2_parts = two_parts(dot(ds2.astype(BF16), kv2).T[:HEAD_DIM])

    for half in range(2):
        dq_pack(half)
    own_copies.append(take_home(1, out_q, HOME_DQ_ROW, HALF, HOME_DQ))
    received(PASS + 1, rows2.at[this_core])
    qg2 = rows2[...].reshape(KEYS, PAIR)
    back = dot_nt(
        jnp.concatenate(
            [jnp.where(few_low, own_kv2, 0.0), jnp.where(few_low, 0.0, own_kv2)], axis=0
        ).astype(BF16),
        qg2,
    )
    scaled_q2 = jnp.where(lane_low, qg2 * jnp.asarray(SCALE, BF16), zero)
    only_g2 = jnp.where(lane_low, zero, qg2)
    at = iota((GROUP * TILE, FEW), 0)
    deal = one_hot(
        (iota((GROUP * TILE, FEW), 1) == (at >> 4) * 4 + (at & (TILE - 1)))
        & ((at & (TILE - 1)) < 4)
    )
    received(STAT, other_stats)
    tiles = []
    for m in range(0, 2 * MATES, 4):
        tiles.append((stats2[m] + stats2[m + 1]) + (stats2[m + 2] + stats2[m + 3]))
    tiles = jnp.concatenate(tiles, axis=1)
    p2 = jnp.exp2(back[:FEW] * TO_EXP2 - tiles[0:1])
    ds2 = p2 * (back[FEW:] - tiles[1:2])
    kv_grad2 = dot(ds2.astype(BF16), scaled_q2) + dot(p2.astype(BF16), only_g2)
    dealt = dot(deal, kv_grad2.astype(BF16)).astype(BF16)
    for r in range(GROUP):
        out_few[r] = dealt[r * TILE : (r + 1) * TILE]
    own_copies.append(take_home(2, out_few, HOME_L2_ROW, TILE, HOME2))

    sent(FEW_OWN, few.at[pl.ds(TILE, (GROUP - 1) * TILE)])
    sent(FEW_PAIRED, few1)
    sent(KV, kv.at[:, pl.ds(HALF, WIDE - HALF), :])
    sent(LEVEL1, peer)
    for c in range(4):
        sent(block_kind(c), block_slots(c))
    sent(GATHER + layer, other_layers)
    sent(ROWS2, other_layers)
    sent(PASS, keys2.at[this_core])
    sent(PASS + 1, rows2.at[this_core])
    sent(STAT, other_stats)

    for done in (received, sent):
        done(HOME_DQ, out_q.at[pl.ds(1, GROUP - 1)])
        done(HOME1, out_l1)
        done(HOME_KV, out_kv.at[pl.ds(1, GROUP - 1)])
    for copy in own_copies:
        copy.wait()
    for done in (received, sent):
        done(HOME2, out_few.at[pl.ds(1, GROUP - 1)])


def finish(off_hbm, fin_hbm, dq_hbm, dk_hbm, dv_hbm, off_ref, fin, held, load_sem, store_sem):
    parts = (
        (HOME_DQ_ROW, HALF),
        (HOME_L2_ROW, TILE),
        (HOME_L1_ROW, HALF),
        (0, ROWS),
    )
    loads = [pltpu.make_async_copy(off_hbm, off_ref, load_sem.at[len(parts)])]
    for i, (first, rows) in enumerate(parts):
        block = (slice(None), pl.ds(first, rows))
        loads.append(pltpu.make_async_copy(fin_hbm.at[block], fin.at[block], load_sem.at[i]))
    for load in loads:
        load.start()
    row = iota((ROWS, ROWS), 0)
    col = iota((ROWS, ROWS), 1)
    merge = one_hot(row == jnp.where(col < HALF, 2 * col, 2 * col - (ROWS - 1)))
    low = iota((ROWS, PAIR), 1) < HEAD_DIM
    half_low = iota((HALF, PAIR), 1) < HEAD_DIM
    tile_row = iota((ROWS, TILE), 0)
    tile_col = iota((ROWS, TILE), 1)
    loads[0].wait()

    def ordered(h, first, second):
        even = off_ref[1, h] == 0
        return jnp.where(even, first, second), jnp.where(even, second, first)

    def ordered_kv(h):
        place = ((off_ref[1, h] + off_ref[2, h]) % 2) * HALF + (off_ref[2, h] >> 1)
        hit = one_hot((tile_row == place + tile_col * 16) & (tile_col < 4))
        level2 = dot(hit, fin[h, HOME_L2_ROW:])
        first = fin[h, :HALF].astype(F32) + fin[h, HOME_L1_ROW : HOME_L1_ROW + HALF].astype(F32) + level2[:HALF]
        second = fin[h, HALF:ROWS].astype(F32) + level2[HALF:]
        return jnp.concatenate(ordered(h, first, second), axis=0)

    def ordered_q(h, side):
        halves = []
        for start in (HOME_DQ_ROW, HOME_DQ_ROW + QUARTER):
            x = fin[h, start : start + QUARTER].astype(F32)
            turned = pltpu.roll(x, HEAD_DIM, 1)
            halves.append(jnp.concatenate([turned, x] if side else [x, turned], axis=0))
        return ordered(h, *halves)

    loads[1].wait()
    stores = []

    def store(i, parts, result):
        for t, x in enumerate(parts):
            lanes = slice(t * PAIR, (t + 1) * PAIR)
            held[i, :, lanes] = dot(merge, x.astype(BF16)).astype(BF16)
        stores.append(pltpu.make_async_copy(held.at[i], result, store_sem.at[i]))
        stores[-1].start()

    parts = []
    for t in range(HEADS // 2):
        a = ordered_q(2 * t, 0)
        b = ordered_q(2 * t + 1, 1)
        both = [jnp.where(half_low, a[i], b[i]) for i in range(2)]
        parts.append(jnp.concatenate(both, axis=0))
    store(0, parts, dq_hbm)
    for load in loads[2:]:
        load.wait()
    heads = [ordered_kv(h) for h in range(HEADS)]
    pairs = [(heads[h], heads[h + 1]) for h in range(0, HEADS, 2)]
    store(1, [jnp.where(low, a, pltpu.roll(b, HEAD_DIM, 1)) for a, b in pairs], dk_hbm)
    store(2, [jnp.where(low, pltpu.roll(a, HEAD_DIM, 1), b) for a, b in pairs], dv_hbm)
    for copy in stores:
        copy.wait()


def local(queries, keys, values, grad_out, offsets):
    width = HEADS * HEAD_DIM
    dma = pltpu.SemaphoreType.DMA

    def low_buffer(*shape):
        return pltpu.VMEM(shape, BF16)

    result = pl.pallas_call(
        kernel,
        out_shape=jax.ShapeDtypeStruct((HEADS, HOME_ROWS, PAIR), BF16),
        in_specs=[pl.BlockSpec(memory_space=pltpu.HBM)] * 5,
        out_specs=pl.BlockSpec(memory_space=pltpu.HBM),
        scratch_shapes=[
            pltpu.SMEM((LEVELS, HEADS), jnp.int32),
            low_buffer(4, ROWS, width),
            low_buffer(HEADS, TILE, PAIR),
            low_buffer(HEADS, 2, HALF, PAIR),
            low_buffer(HEADS, 2, HALF, PAIR),
            low_buffer(GROUP * TILE, PAIR),
            low_buffer(GROUP * TILE, PAIR),
            low_buffer(2, WIDE, PAIR),
            low_buffer(2, WIDE, PAIR),
            low_buffer(WIDE, PAIR),
            low_buffer(2 * MATES, FEW, PAIR),
            low_buffer(2 * MATES, FEW, PAIR),
            pltpu.VMEM((2 * MATES, 2, PAIR), F32),
            low_buffer(HEAD_DIM, KEYS + WIDE),
            low_buffer(GROUP, ROWS, PAIR),
            low_buffer(GROUP, HALF, PAIR),
            low_buffer(WIDE, PAIR),
            low_buffer(GROUP, TILE, PAIR),
            pltpu.VMEM((4, KEYS + WIDE, COLS), F32),
            pltpu.VMEM((4, KEYS + WIDE, COLS), F32),
            low_buffer(4, KEYS + WIDE, COLS),
            pltpu.VMEM((2, HEAD_DIM, WIDE), F32),
            pltpu.VMEM((KEYS + WIDE, PAIR), F32),
            dma((KINDS,)),
            dma((KINDS,)),
            dma((2,)),
            dma((3,)),
            pltpu.SemaphoreType.REGULAR,
        ],
        compiler_params=pltpu.CompilerParams(
            collective_id=0, has_side_effects=True, vmem_limit_bytes=63 * 1024 * 1024
        ),
    )(offsets, queries, keys, values, grad_out)
    one = jax.ShapeDtypeStruct((ROWS, width), BF16)
    hbm = pl.BlockSpec(memory_space=pltpu.HBM)
    return pl.pallas_call(
        finish,
        out_shape=(one, one, one),
        in_specs=[hbm, hbm],
        out_specs=(hbm, hbm, hbm),
        scratch_shapes=[
            pltpu.SMEM((LEVELS, HEADS), jnp.int32),
            low_buffer(HEADS, HOME_ROWS, PAIR),
            low_buffer(3, ROWS, width),
            dma((5,)),
            dma((3,)),
        ],
        compiler_params=pltpu.CompilerParams(vmem_limit_bytes=63 * 1024 * 1024),
    )(offsets, result)


def solution(mesh):
    rows = P(("ctxa", "ctxb"), None)
    return jax.shard_map(
        local,
        mesh=mesh,
        in_specs=(rows, rows, rows, rows, P()),
        out_specs=(rows, rows, rows),
        check_vma=False,
    )
```

```python
import math

import jax
import jax.numpy as jnp
from jax import lax
from jax.experimental import pallas as pl
from jax.experimental.pallas import tpu as pltpu
from jax.sharding import PartitionSpec as P

HEADS = 8
HEAD_DIM = 64
KEYS = 1024
LEVELS = 3
ROWS = 128
HALF = ROWS // 2
GROUP = 8
MATES = 16
WIDE = 512
FEW = 32
TILE = 16
PAIR = 2 * HEAD_DIM
SCALE = HEAD_DIM ** (-0.5)
TO_EXP2 = SCALE * math.log2(math.e)
LOWEST = -1e30
MESH = pl.DeviceIdType.MESH
F32 = jnp.float32
BF16 = jnp.bfloat16
COLS = 256
SLOTS = COLS // HALF
DEEP = 128
QUARTER = HALF // 2
HOME_L1_ROW = ROWS
HOME_DQ_ROW = HOME_L1_ROW + HALF
HOME_L2_ROW = HOME_DQ_ROW + HALF
HOME_ROWS = HOME_L2_ROW + TILE
KINDS = 24
(
    FEW_OWN,
    FEW_PAIRED,
    KV,
    LEVEL1,
    QG,
    GATHER,
    ROWS2,
    PASS,
    STAT,
    HOME_DQ,
    HOME_KV,
    HOME1,
    HOME2,
) = (0, 1, 2, 3, 4, 8, 16, 17, 19, 20, 21, 22, 23)
FAR_FIRST = (6, 2, 5, 7, 4, 1, 3)
LAYERS = 8
NEAR_LAYERS = (2, 6, 1, 7)
LAYERS_FAR_FIRST = (4, 3, 5, 2, 6, 1, 7)
MATES_FAR_FIRST = (9, 8, 7, 10, 6, 11, 5, 12, 4, 13, 3, 14, 2, 15, 1)


def dot(x, y):
    return jnp.dot(x, y, preferred_element_type=F32)


def dot_nt(x, y):
    return lax.dot_general(x, y, (((1,), (1,)), ((), ())), preferred_element_type=F32)


def iota(shape, dim):
    return lax.broadcasted_iota(jnp.int32, shape, dim)


def one_hot(hit):
    return hit.astype(F32).astype(BF16)


def two_parts(x):
    high = x.astype(BF16)
    return high, (x - high.astype(F32)).astype(BF16)


def fold8(x, op):
    parts = [x[8 * i : 8 * i + 8] for i in range(x.shape[0] // 8)]
    while len(parts) > 1:
        parts = [op(parts[i], parts[i + 1]) for i in range(0, len(parts), 2)]
    return parts[0]


def kernel(
    off_hbm,
    q_hbm,
    k_hbm,
    v_hbm,
    g_hbm,
    fin,
    off_ref,
    in_ref,
    send_few,
    send_kv,
    send_qg,
    few,
    few1,
    kv,
    qg,
    peer,
    keys2,
    rows2,
    stats2,
    k_t,
    out_kv,
    out_q,
    out_l1,
    out_few,
    score,
    dprob,
    dsc,
    dq_t,
    acc,
    send_sem,
    recv_sem,
    load_sem,
    own_sem,
    hop_sem,
):
    loads = [
        pltpu.make_async_copy(src, in_ref.at[i], load_sem.at[0])
        for i, src in enumerate((k_hbm, v_hbm, q_hbm, g_hbm))
    ]
    loads.append(pltpu.make_async_copy(off_hbm, off_ref, load_sem.at[1]))
    for load in loads:
        load.start()

    major = lax.axis_index("ctxa")
    minor = lax.axis_index("ctxb")
    head = minor % GROUP
    mate = (major // 2) * 4 + minor // GROUP

    def member(dx, dy):
        x = (head % 4 + dx) % 4
        y = (head // 4 + dy) % 2
        return y * 4 + x

    def at_head(other):
        return (major, (minor // GROUP) * GROUP + other)

    def at_mate(other, flip=0):
        return ((other // 4) * 2 + (major + flip) % 2, (other % 4) * GROUP + head)

    layer = mate // 2

    def at_layer(other):
        return ((other // 2) * 2 + major % 2, (other % 2) * (2 * GROUP) + minor % (2 * GROUP))

    ahead = [member(r % 4, r // 4) for r in range(GROUP)]
    behind = [member(4 - r % 4, r // 4) for r in range(GROUP)]
    sibling = (major + 1 - 2 * (major % 2), minor)
    paired = minor // GROUP + 1 - 2 * ((minor // GROUP) % 2)

    def at_paired(other):
        return (major, paired * GROUP + other)

    def send(src, dst, kind, device):
        pltpu.make_async_remote_copy(
            src_ref=src,
            dst_ref=dst,
            send_sem=send_sem.at[kind],
            recv_sem=recv_sem.at[kind],
            device_id=device,
            device_id_type=MESH,
        ).start()

    def received(kind, amount):
        pltpu.make_async_copy(amount, amount, recv_sem.at[kind]).wait()

    def sent(kind, amount):
        pltpu.make_async_copy(amount, amount, send_sem.at[kind]).wait()

    barrier = pltpu.get_barrier_semaphore()

    def greet(device):
        pl.semaphore_signal(barrier, inc=1, device_id=device, device_id_type=MESH)

    for r in FAR_FIRST:
        greet(at_head(ahead[r]))
    for r in (*FAR_FIRST, 0):
        greet(at_paired(behind[r]))
    for r in NEAR_LAYERS:
        greet(at_layer((layer + r) % LAYERS))
    greet(sibling)
    row = iota((ROWS, ROWS), 0)
    col = iota((ROWS, ROWS), 1)
    split = one_hot(col == jnp.where(row < HALF, 2 * row, 2 * row - (ROWS - 1)))
    low = iota((ROWS, PAIR), 1) < HEAD_DIM

    pltpu.make_async_copy(in_ref, in_ref, load_sem.at[0]).wait()
    loads[4].wait()
    order = [[None, None] for _ in range(HEADS)]
    for which, packed in enumerate((send_kv, send_qg)):
        x_all = dot(split, in_ref[2 * which])
        y_all = dot(split, in_ref[2 * which + 1])
        for t in range(HEADS // 2):
            x = x_all[:, t * PAIR : (t + 1) * PAIR]
            y = y_all[:, t * PAIR : (t + 1) * PAIR]
            for h, both in (
                (2 * t, jnp.where(low, x, pltpu.roll(y, HEAD_DIM, 1))),
                (2 * t + 1, jnp.where(low, pltpu.roll(x, HEAD_DIM, 1), y)),
            ):
                even = off_ref[1, h] == 0
                first = jnp.where(even, both[:HALF], both[HALF:]).astype(BF16)
                second = jnp.where(even, both[HALF:], both[:HALF]).astype(BF16)
                packed[h, 0] = first
                packed[h, 1] = second
                order[h][which] = [first, second]
    tile_row = iota((TILE, 2 * ROWS), 0)
    tile_col = iota((TILE, 2 * ROWS), 1)
    wanted = (tile_row >> 2) * ROWS + (tile_row & 3) * 16
    for h in range(HEADS):
        place = ((off_ref[1, h] + off_ref[2, h]) % 2) * HALF + (off_ref[2, h] >> 1)
        hit = one_hot((tile_col == wanted + place) & (tile_row < 8))
        send_few[h] = dot(hit, jnp.concatenate(order[h][0] + order[h][1], axis=0)).astype(BF16)

    pl.semaphore_wait(barrier, GROUP - 1 + GROUP + len(NEAR_LAYERS) + 1)

    for r in FAR_FIRST:
        tile = few.at[pl.ds(r * TILE, TILE), :]
        send(send_few.at[ahead[r]], tile, FEW_OWN, at_head(ahead[r]))
    for r in (*FAR_FIRST, 0):
        tile = few1.at[pl.ds(r * TILE, TILE), :]
        send(send_few.at[ahead[r]], tile, FEW_PAIRED, at_paired(ahead[r]))
    for r in NEAR_LAYERS[:2]:
        pl.semaphore_signal(
            hop_sem,
            inc=1,
            device_id=at_layer((layer + r) % LAYERS),
            device_id_type=MESH,
        )
    for r in FAR_FIRST:
        slot = kv.at[:, pl.ds(r * HALF, HALF), :]
        send(send_kv.at[ahead[r]], slot, KV, at_head(ahead[r]))
    for r in (*FAR_FIRST, 0):
        slot = peer.at[pl.ds(r * HALF, HALF), :]
        send(send_kv.at[ahead[r], 0], slot, LEVEL1, at_paired(ahead[r]))

    def block_kind(c):
        return QG + c

    for half in (0, 1):
        for r in FAR_FIRST:
            slot = qg.at[half, pl.ds(r * HALF, HALF), :]
            kind = block_kind(2 * half + r // SLOTS)
            send(send_qg.at[ahead[r], half], slot, kind, at_head(ahead[r]))
    few[:TILE] = send_few[head]
    kv[:, :HALF] = send_kv[head]
    qg[:, :HALF] = send_qg[head]

    off1 = off_ref[1, head]
    off2 = off_ref[2, head]
    inside = (off1 + off2) % 2 == 0
    base = jnp.where(inside, 0, WIDE) + (off2 >> 1)
    at = iota((FEW, KEYS), 0)
    pick = iota((FEW, KEYS), 1) == base + (at >> 2) * HALF + (at & 3) * 16
    at = iota((KEYS, FEW), 1)
    pick_t = one_hot(iota((KEYS, FEW), 0) == base + (at >> 2) * HALF + (at & 3) * 16)
    pick_low = one_hot(pick)
    at = iota((2 * FEW, GROUP * TILE), 0)
    gather = one_hot(
        iota((2 * FEW, GROUP * TILE), 1)
        == ((at % FEW) >> 2) * TILE + (at & 3) + jnp.where(at < FEW, 0, 4)
    )
    pl.semaphore_wait(hop_sem, 2)
    received(FEW_OWN, few.at[pl.ds(TILE, (GROUP - 1) * TILE)])
    received(FEW_PAIRED, few1)
    picked = dot(gather, few[...])
    picked1 = dot(gather, few1[...])
    own_kv2 = picked[:FEW]
    own_qg2 = picked[FEW:]
    mate1 = mate + 1 - 2 * (mate % 2)
    keys2[mate] = own_kv2.astype(BF16)
    rows2[mate] = own_qg2.astype(BF16)
    keys2[mate1] = picked1[:FEW].astype(BF16)
    rows2[mate1] = picked1[FEW:].astype(BF16)
    block = keys2.at[pl.ds(layer * 2, 2)]
    for r in LAYERS_FAR_FIRST:
        send(block, block, GATHER + layer, at_layer((layer + r) % LAYERS))
    send(block, keys2.at[pl.ds(MATES + layer * 2, 2)], PASS, sibling)
    other_layers = keys2.at[pl.ds(0, MATES - 2)]
    this_core = pl.ds(0, MATES)
    that_core = pl.ds(MATES, MATES)

    received(KV, kv.at[:, pl.ds(HALF, WIDE - HALF), :])
    lane_low = iota((1, PAIR), 1) < HEAD_DIM
    zero = jnp.zeros((), BF16)
    kv_all = kv[...].reshape(KEYS, PAIR)

    def block_slots(c):
        slots = SLOTS if c % 2 else SLOTS - 1
        return qg.at[c // 2, pl.ds(WIDE - COLS, slots * HALF), :]

    def key_rows(j):
        if j < KEYS:
            return kv[j // WIDE, j % WIDE : j % WIDE + DEEP]
        return peer[j - KEYS : j - KEYS + DEEP]

    def stats(c):
        half = c // 2
        first = (c % 2) * COLS
        across = qg[half, first : first + COLS, :].T
        across_low = iota((PAIR, COLS), 0) < HEAD_DIM
        across_q = jnp.where(across_low, across, zero)
        across_g = jnp.where(across_low, zero, across)
        steps = range(0, depth_of(c), DEEP)
        high8 = jnp.full((8, COLS), LOWEST, F32)
        for j in steps:
            s = dot(key_rows(j), across_q) * TO_EXP2
            score[c, j : j + DEEP] = s
            high8 = jnp.maximum(high8, fold8(s, jnp.maximum))
        high = jnp.max(high8, axis=0, keepdims=True)
        sum8 = jnp.zeros((8, COLS), F32)
        dot8 = jnp.zeros((8, COLS), F32)
        for j in steps:
            e = jnp.exp2(score[c, j : j + DEEP] - high)
            score[c, j : j + DEEP] = e
            d = dot(key_rows(j), across_g)
            dprob[c, j : j + DEEP] = d
            sum8 = sum8 + weight(c, j) * fold8(e, jnp.add)
            dot8 = dot8 + weight(c, j) * fold8(e * d, jnp.add)
        return (
            high,
            jnp.sum(sum8, axis=0, keepdims=True),
            jnp.sum(dot8, axis=0, keepdims=True),
        )

    def depth_of(c):
        return KEYS + WIDE if c < 2 else KEYS

    def weight(c, j):
        return 2.0 if c < 2 and j < WIDE else 1.0

    received(LEVEL1, peer)
    peer_all = peer[...]
    for i in range(LAYERS - 1):
        other = i + (i + LAYERS - layer) // LAYERS
        block = keys2.at[pl.ds(other * 2, 2)]
        received(GATHER + other, block)
        send(block, keys2.at[pl.ds(MATES + other * 2, 2)], PASS, sibling)
    few_low = iota((FEW, PAIR), 1) < HEAD_DIM
    both2 = jnp.concatenate(
        [jnp.where(few_low, own_qg2, 0.0), jnp.where(few_low, 0.0, own_qg2)], axis=0
    ).astype(BF16)
    here = dot_nt(both2, kv_all)
    near = dot_nt(both2, peer_all)
    s_here = here[:FEW] * TO_EXP2
    s_near = jnp.where(inside, near[:FEW] * TO_EXP2, LOWEST)
    twice = jnp.where((iota((FEW, KEYS), 1) < WIDE) & inside, 2.0, 1.0)
    high_own = jnp.maximum(
        jnp.max(s_here, axis=1, keepdims=True), jnp.max(s_near, axis=1, keepdims=True)
    )
    e_here = jnp.exp2(s_here - high_own) * twice
    e_near = jnp.exp2(s_near - high_own)
    sum_own = jnp.sum(e_here, axis=1, keepdims=True) + jnp.sum(e_near, axis=1, keepdims=True)
    dot_own = jnp.sum(e_here * here[FEW:], axis=1, keepdims=True) + jnp.sum(
        e_near * near[FEW:], axis=1, keepdims=True
    )
    block = rows2.at[pl.ds(layer * 2, 2)]
    for r in LAYERS_FAR_FIRST:
        send(block, block, ROWS2, at_layer((layer + r) % LAYERS))
    for c in (0, 1):
        received(block_kind(c), block_slots(c))
    found = [stats(0), stats(1)]
    k_t[:, :KEYS] = kv_all.T[:HEAD_DIM]
    k_t[:, KEYS:] = peer_all.T[:HEAD_DIM]
    received(PASS, keys2.at[this_core])

    kv2 = keys2[...].reshape(KEYS, PAIR)
    far = dot_nt(both2, kv2)
    s2 = far[:FEW] * TO_EXP2
    d2 = far[FEW:]
    high2 = jnp.maximum(high_own, jnp.max(s2, axis=1, keepdims=True))
    e2 = jnp.exp2(s2 - high2)
    sum2 = jnp.sum(e2, axis=1, keepdims=True)
    dot2 = jnp.sum(e2 * d2, axis=1, keepdims=True)
    shift = jnp.exp2(high_own - high2)
    total2 = sum2 + shift * sum_own
    product2 = dot2 + shift * dot_own
    lse2 = high2 + jnp.log(total2) * math.log2(math.e)
    delta2 = product2 / total2
    lanes = iota((FEW, PAIR), 1) == (mate % 4) * FEW + iota((FEW, PAIR), 0)
    stats2[mate] = jnp.concatenate(
        [
            jnp.sum(jnp.where(lanes, lse2, 0.0), axis=0, keepdims=True),
            jnp.sum(jnp.where(lanes, delta2, 0.0), axis=0, keepdims=True),
        ],
        axis=0,
    )
    stat_block = stats2.at[mate]
    stat_block1 = stats2.at[MATES + mate]
    for r in MATES_FAR_FIRST:
        send(stat_block, stat_block, STAT, at_mate((mate + r) % MATES))
        send(stat_block, stat_block1, STAT, at_mate((mate + r) % MATES, 1))
    send(stat_block, stat_block1, STAT, sibling)
    other_stats = stats2.at[pl.ds(0, 2 * MATES - 1)]
    high2_row = jnp.max(jnp.where(pick, high2, LOWEST), axis=0, keepdims=True)
    sum2_row = jnp.sum(jnp.where(pick, sum2, 0.0), axis=0, keepdims=True)
    dot2_row = jnp.sum(jnp.where(pick, dot2, 0.0), axis=0, keepdims=True)

    def grads(c, own):
        columns = slice(c * COLS, (c + 1) * COLS)
        high, total, product = own
        top = jnp.maximum(high, high2_row[:, columns])
        factor = jnp.exp2(high - top)
        factor2 = jnp.exp2(high2_row[:, columns] - top)
        inverse = 1.0 / (factor * total + factor2 * sum2_row[:, columns])
        delta = (factor * product + factor2 * dot2_row[:, columns]) * inverse
        factor = factor * inverse
        mine = qg[c // 2, (c % 2) * COLS : (c % 2 + 1) * COLS, :]
        scaled_q = jnp.where(lane_low, mine * jnp.asarray(SCALE, BF16), zero)
        only_g = jnp.where(lane_low, zero, mine)
        depth = depth_of(c)
        for j in range(0, depth, DEEP):
            p = score[c, j : j + DEEP] * (weight(c, j) * factor)
            ds = (p * (dprob[c, j : j + DEEP] - delta)).astype(BF16)
            dsc[c, j : j + DEEP] = ds
            added = dot(ds, scaled_q) + dot(p.astype(BF16), only_g)
            acc[j : j + DEEP] = added if c == 0 else acc[j : j + DEEP] + added
        dq_t[c // 2, :, (c % 2) * COLS : (c % 2 + 1) * COLS] = dot(k_t[:, :depth], dsc[c, :depth])

    def dq_pack(half):
        columns = slice(half * WIDE, (half + 1) * WIDE)
        dq = dq_t[half] + dot(dq2_parts[0], pick_low[:, columns])
        dq = (dq + dot(dq2_parts[1], pick_low[:, columns])) * SCALE
        lanes_low = iota((QUARTER, PAIR), 1) < HEAD_DIM
        for i in range(0, WIDE, PAIR):
            two = jnp.concatenate([dq[:, i : i + PAIR], dq[:, i : i + PAIR]], axis=0).T
            for b in range(2):
                rows = two[b * HALF : (b + 1) * HALF]
                packed = jnp.where(lanes_low, rows[:QUARTER], rows[QUARTER:]).astype(BF16)
                out_q[i // HALF + b, half * QUARTER : (half + 1) * QUARTER] = packed

    grads(0, found[0])
    grads(1, found[1])
    out_l1[...] = acc[KEYS:].astype(BF16)
    for r in (*FAR_FIRST, 0):
        slot = out_l1.at[pl.ds(r * HALF, HALF), :]
        send(slot, fin.at[head, pl.ds(HOME_L1_ROW, HALF)], HOME1, at_paired(behind[r]))

    def take_home(i, src, first, rows, kind):
        place = fin.at[head, pl.ds(first, rows)]
        for r in FAR_FIRST:
            send(src.at[r], place, kind, at_head(behind[r]))
        copy = pltpu.make_async_copy(src.at[0], place, own_sem.at[i])
        copy.start()
        return copy

    received(ROWS2, other_layers)
    send(rows2.at[this_core], rows2.at[that_core], PASS + 1, sibling)
    for c in (2, 3):
        received(block_kind(c), block_slots(c))
    found += [stats(2), stats(3)]
    grads(2, found[2])
    grads(3, found[3])
    for r in range(GROUP):
        for half in range(2):
            rows = slice(half * WIDE + r * HALF, half * WIDE + (r + 1) * HALF)
            out_kv[r, half * HALF : (half + 1) * HALF] = acc[rows].astype(BF16)
    own_copies = [take_home(0, out_kv, 0, ROWS, HOME_KV)]
    ds2 = jnp.exp2(s2 - lse2) * (d2 - delta2)
    dq2_parts = two_parts(dot(ds2.astype(BF16), kv2).T[:HEAD_DIM])

    for half in range(2):
        dq_pack(half)
    own_copies.append(take_home(1, out_q, HOME_DQ_ROW, HALF, HOME_DQ))
    received(PASS + 1, rows2.at[this_core])
    qg2 = rows2[...].reshape(KEYS, PAIR)
    back = dot_nt(
        jnp.concatenate(
            [jnp.where(few_low, own_kv2, 0.0), jnp.where(few_low, 0.0, own_kv2)], axis=0
        ).astype(BF16),
        qg2,
    )
    scaled_q2 = jnp.where(lane_low, qg2 * jnp.asarray(SCALE, BF16), zero)
    only_g2 = jnp.where(lane_low, zero, qg2)
    at = iota((GROUP * TILE, FEW), 0)
    deal = one_hot(
        (iota((GROUP * TILE, FEW), 1) == (at >> 4) * 4 + (at & (TILE - 1)))
        & ((at & (TILE - 1)) < 4)
    )
    received(STAT, other_stats)
    tiles = []
    for m in range(0, 2 * MATES, 4):
        tiles.append((stats2[m] + stats2[m + 1]) + (stats2[m + 2] + stats2[m + 3]))
    tiles = jnp.concatenate(tiles, axis=1)
    p2 = jnp.exp2(back[:FEW] * TO_EXP2 - tiles[0:1])
    ds2 = p2 * (back[FEW:] - tiles[1:2])
    kv_grad2 = dot(ds2.astype(BF16), scaled_q2) + dot(p2.astype(BF16), only_g2)
    dealt = dot(deal, kv_grad2.astype(BF16)).astype(BF16)
    for r in range(GROUP):
        out_few[r] = dealt[r * TILE : (r + 1) * TILE]
    own_copies.append(take_home(2, out_few, HOME_L2_ROW, TILE, HOME2))

    sent(FEW_OWN, few.at[pl.ds(TILE, (GROUP - 1) * TILE)])
    sent(FEW_PAIRED, few1)
    sent(KV, kv.at[:, pl.ds(HALF, WIDE - HALF), :])
    sent(LEVEL1, peer)
    for c in range(4):
        sent(block_kind(c), block_slots(c))
    sent(GATHER + layer, other_layers)
    sent(ROWS2, other_layers)
    sent(PASS, keys2.at[this_core])
    sent(PASS + 1, rows2.at[this_core])
    sent(STAT, other_stats)

    for done in (received, sent):
        done(HOME_DQ, out_q.at[pl.ds(1, GROUP - 1)])
        done(HOME1, out_l1)
        done(HOME_KV, out_kv.at[pl.ds(1, GROUP - 1)])
    for copy in own_copies:
        copy.wait()
    for done in (received, sent):
        done(HOME2, out_few.at[pl.ds(1, GROUP - 1)])


def finish(off_hbm, fin_hbm, dq_hbm, dk_hbm, dv_hbm, off_ref, fin, held, load_sem, store_sem):
    parts = (
        (HOME_DQ_ROW, HALF),
        (HOME_L2_ROW, TILE),
        (HOME_L1_ROW, HALF),
        (0, ROWS),
    )
    loads = [pltpu.make_async_copy(off_hbm, off_ref, load_sem.at[len(parts)])]
    for i, (first, rows) in enumerate(parts):
        block = (slice(None), pl.ds(first, rows))
        loads.append(pltpu.make_async_copy(fin_hbm.at[block], fin.at[block], load_sem.at[i]))
    for load in loads:
        load.start()
    row = iota((ROWS, ROWS), 0)
    col = iota((ROWS, ROWS), 1)
    merge = one_hot(row == jnp.where(col < HALF, 2 * col, 2 * col - (ROWS - 1)))
    low = iota((ROWS, PAIR), 1) < HEAD_DIM
    half_low = iota((HALF, PAIR), 1) < HEAD_DIM
    tile_low = iota((TILE, PAIR), 1) < HEAD_DIM
    loads[0].wait()

    def ordered(h, first, second):
        even = off_ref[1, h] == 0
        return jnp.where(even, first, second), jnp.where(even, second, first)

    def merge_with_level2(t):
        to = iota((ROWS, ROWS + 2 * TILE), 0)
        at = iota((ROWS, ROWS + 2 * TILE), 1)
        hit = to == jnp.where(at < HALF, 2 * at, 2 * at - (ROWS - 1))
        hit = hit & (at < ROWS)
        for i in range(2):
            tile = at - (ROWS + i * TILE)
            row = off_ref[2, 2 * t + i] + tile * FEW
            hit = hit | ((to == row) & (tile >= 0) & (tile < 4))
        return one_hot(hit)

    def ordered_kv(h):
        first = fin[h, :HALF].astype(F32) + fin[h, HOME_L1_ROW : HOME_L1_ROW + HALF].astype(F32)
        return jnp.concatenate(ordered(h, first, fin[h, HALF:ROWS].astype(F32)), axis=0)

    def beside(a, b, is_low):
        dk = jnp.where(is_low, a, pltpu.roll(b, HEAD_DIM, 1))
        return dk, jnp.where(is_low, pltpu.roll(a, HEAD_DIM, 1), b)

    def with_level2(t):
        base = beside(ordered_kv(2 * t), ordered_kv(2 * t + 1), low)
        a = fin[2 * t, HOME_L2_ROW:].astype(F32)
        b = fin[2 * t + 1, HOME_L2_ROW:].astype(F32)
        none = jnp.zeros_like(a)
        few_a = beside(a, none, tile_low)
        few_b = beside(none, b, tile_low)
        return [
            jnp.concatenate([base[i], few_a[i], few_b[i]], axis=0).astype(BF16) for i in range(2)
        ]

    def ordered_q(h, side):
        halves = []
        for start in (HOME_DQ_ROW, HOME_DQ_ROW + QUARTER):
            x = fin[h, start : start + QUARTER].astype(F32)
            turned = pltpu.roll(x, HEAD_DIM, 1)
            halves.append(jnp.concatenate([turned, x] if side else [x, turned], axis=0))
        return ordered(h, *halves)

    merges = [merge_with_level2(t) for t in range(HEADS // 2)]
    loads[1].wait()
    stores = []

    def store(i, parts, left, result):
        for t, x in enumerate(parts):
            lanes = slice(t * PAIR, (t + 1) * PAIR)
            held[i, :, lanes] = dot(left[t], x).astype(BF16)
        stores.append(pltpu.make_async_copy(held.at[i], result, store_sem.at[i]))
        stores[-1].start()

    parts = []
    for t in range(HEADS // 2):
        a = ordered_q(2 * t, 0)
        b = ordered_q(2 * t + 1, 1)
        both = [jnp.where(half_low, a[i], b[i]) for i in range(2)]
        parts.append(jnp.concatenate(both, axis=0).astype(BF16))
    store(0, parts, [merge] * (HEADS // 2), dq_hbm)
    for load in loads[2:]:
        load.wait()
    pairs = [with_level2(t) for t in range(HEADS // 2)]
    store(1, [pair[0] for pair in pairs], merges, dk_hbm)
    store(2, [pair[1] for pair in pairs], merges, dv_hbm)
    for copy in stores:
        copy.wait()


def local(queries, keys, values, grad_out, offsets):
    width = HEADS * HEAD_DIM
    dma = pltpu.SemaphoreType.DMA

    def low_buffer(*shape):
        return pltpu.VMEM(shape, BF16)

    result = pl.pallas_call(
        kernel,
        out_shape=jax.ShapeDtypeStruct((HEADS, HOME_ROWS, PAIR), BF16),
        in_specs=[pl.BlockSpec(memory_space=pltpu.HBM)] * 5,
        out_specs=pl.BlockSpec(memory_space=pltpu.HBM),
        scratch_shapes=[
            pltpu.SMEM((LEVELS, HEADS), jnp.int32),
            low_buffer(4, ROWS, width),
            low_buffer(HEADS, TILE, PAIR),
            low_buffer(HEADS, 2, HALF, PAIR),
            low_buffer(HEADS, 2, HALF, PAIR),
            low_buffer(GROUP * TILE, PAIR),
            low_buffer(GROUP * TILE, PAIR),
            low_buffer(2, WIDE, PAIR),
            low_buffer(2, WIDE, PAIR),
            low_buffer(WIDE, PAIR),
            low_buffer(2 * MATES, FEW, PAIR),
            low_buffer(2 * MATES, FEW, PAIR),
            pltpu.VMEM((2 * MATES, 2, PAIR), F32),
            low_buffer(HEAD_DIM, KEYS + WIDE),
            low_buffer(GROUP, ROWS, PAIR),
            low_buffer(GROUP, HALF, PAIR),
            low_buffer(WIDE, PAIR),
            low_buffer(GROUP, TILE, PAIR),
            pltpu.VMEM((4, KEYS + WIDE, COLS), F32),
            pltpu.VMEM((4, KEYS + WIDE, COLS), F32),
            low_buffer(4, KEYS + WIDE, COLS),
            pltpu.VMEM((2, HEAD_DIM, WIDE), F32),
            pltpu.VMEM((KEYS + WIDE, PAIR), F32),
            dma((KINDS,)),
            dma((KINDS,)),
            dma((2,)),
            dma((3,)),
            pltpu.SemaphoreType.REGULAR,
        ],
        compiler_params=pltpu.CompilerParams(
            collective_id=0, has_side_effects=True, vmem_limit_bytes=63 * 1024 * 1024
        ),
    )(offsets, queries, keys, values, grad_out)
    one = jax.ShapeDtypeStruct((ROWS, width), BF16)
    hbm = pl.BlockSpec(memory_space=pltpu.HBM)
    return pl.pallas_call(
        finish,
        out_shape=(one, one, one),
        in_specs=[hbm, hbm],
        out_specs=(hbm, hbm, hbm),
        scratch_shapes=[
            pltpu.SMEM((LEVELS, HEADS), jnp.int32),
            low_buffer(HEADS, HOME_ROWS, PAIR),
            low_buffer(3, ROWS, width),
            dma((5,)),
            dma((3,)),
        ],
        compiler_params=pltpu.CompilerParams(vmem_limit_bytes=63 * 1024 * 1024),
    )(offsets, result)


def solution(mesh):
    rows = P(("ctxa", "ctxb"), None)
    return jax.shard_map(
        local,
        mesh=mesh,
        in_specs=(rows, rows, rows, rows, P()),
        out_specs=(rows, rows, rows),
        check_vma=False,
    )
```
